32 devices in a mesh: grp: 1, gx: 16 (over z, y, x), gz: 2 (over core).
Axes of the slice: x: 2, y: 2, z: 4, core: 2. Of those that a mesh axis runs over, the one named last changes fastest.
Arguments:
- field: bfloat16 [20, 32, 32, 2048], P(None, ('grp', 'gx'), 'gz'), may hold values from -6 to 6
- cotangent: bfloat16 [20, 32, 32, 2048], P(None, ('grp', 'gx'), 'gz'), may hold values from -6 to 6
- spec_weight: bfloat16 [2, 20, 20, 192, 384], P(None, None, None, 'gx', 'gz'), may hold values from -9 to 9
- mix_weight: bfloat16 [20, 20], replicated, may hold values from -1.25 to 1.25
Outputs:
- field_grad: bfloat16 [20, 32, 32, 2048], P(None, ('grp', 'gx'), 'gz')
- spec_grad: float32 [2, 20, 20, 192, 384], P('grp', None, None, 'gx', 'gz')
- mix_grad: float32 [20, 20], P('grp')
The draws below stay inside these ranges and needn't reach their ends.
All inputs are finite; a program needn't handle non-finite values.
Results may differ from the reference program's by a relative error of at most 0.018.
Values may be sent and summed in bfloat16 or wider, within the bound.
No kernel may reach another device: no remote copies, remote signals or barrier semaphores. Data moves between devices by JAX's collectives and lax.ppermute only.
A program may use at most 128 MiB of HBM per device.

```python
import math
import jax
import jax.numpy as jnp
from jax import lax

CH = 20
MX = 24
MY = 24
MZ = 16
MT = 8
NY = 128
NSTEP = 16
NX = 32
NZ = 32
MS = 192
NYT = 2048


def block_scale(stream_key, dims, split, low, largest):
    level = 1.0
    for position, shards_of in split:
        draws = jax.random.uniform(jax.random.fold_in(jax.random.fold_in(stream_key, 6), position), (shards_of,), jnp.float32, low / len(split), largest / len(split))
        level = level * jnp.repeat(jnp.exp(draws), dims[position] // shards_of).reshape((-1,) + (1,) * (len(dims) - 1 - position))
    return level


def gaussian(own_key, shape, width, bound, shards=(), kind=jnp.bfloat16):
    values = width * jax.random.normal(own_key, shape, jnp.float32)
    if shards:
        values = values * block_scale(own_key, shape, shards, -0.22, 0.18)
    return jnp.clip(values, -bound, bound).astype(kind)


def setup_inputs(seed: int = 0, part: int = 0) -> dict:
    arg_keys = jax.random.split(jax.random.key(seed), 5)
    part_splits = jax.random.split(jax.random.fold_in(arg_keys[4], part), 5)
    return {
        "field": gaussian(part_splits[0], (CH, NX, NZ, NYT), 1.0, 6.0, ((1, 16), (2, 2))),
        "cotangent": gaussian(part_splits[1], (CH, NX, NZ, NYT), 1.0, 6.0, ((1, 16), (2, 2))),
        "spec_weight": gaussian(arg_keys[2], (2, CH, CH, MS, MX * MZ), 1.5, 9.0, ((3, 16), (4, 2))),
        "mix_weight": gaussian(arg_keys[3], (CH, CH), CH ** -0.5, 1.25),
    }


def mode_angles(length, count, one_sided):
    cells = jnp.arange(length, dtype=jnp.int32)
    ranks = jnp.arange(count, dtype=jnp.int32)
    if one_sided:
        freqs = ranks
    else:
        freqs = jnp.where(ranks < count // 2, ranks, ranks - count)
    wrapped = jnp.mod(cells[:, None] * freqs[None, :], length)
    return wrapped.astype(jnp.float32) * (2.0 * math.pi / length)

def pair_table(angles, conjugate):
    cosine = jnp.cos(angles).astype(jnp.bfloat16)
    sine = jnp.sin(angles).astype(jnp.bfloat16)
    if conjugate:
        rows = [jnp.stack([cosine, sine], -1), jnp.stack([-sine, cosine], -1)]
    else:
        rows = [jnp.stack([cosine, -sine], -1), jnp.stack([sine, cosine], -1)]
    return jnp.stack(rows, 1)

def plane_table(y_len, t_len, y_modes, t_modes):
    y_angle = mode_angles(y_len, y_modes, False)
    t_angle = mode_angles(t_len, t_modes, True)
    total = (y_angle[:, None, :, None] + t_angle[None, :, None, :]).reshape(y_len * t_len, y_modes * t_modes)
    return jnp.concatenate([jnp.cos(total), -jnp.sin(total)], 1).astype(jnp.bfloat16)

def as_float(value):
    return value.astype(jnp.float32)

def to_modes(data, plane, table_x, table_z):
    chans, x_len, z_len, plane_len = data.shape
    spectra = jnp.dot(data.reshape(-1, plane_len), plane, preferred_element_type=jnp.float32)
    spectra = spectra.reshape(chans, x_len, z_len, 2, -1).astype(jnp.bfloat16)
    along_x = jnp.einsum('cxzps,xpkq->ckzqs', as_float(spectra), as_float(table_x), precision=lax.Precision.HIGHEST).astype(jnp.bfloat16)
    return jnp.einsum('ckzps,zplq->cklqs', as_float(along_x), as_float(table_z), precision=lax.Precision.HIGHEST).astype(jnp.bfloat16)

def to_field(modes, plane, inverse_x, inverse_z, scale):
    along_z = jnp.einsum('cklps,zplq->ckzqs', as_float(modes), as_float(inverse_z), precision=lax.Precision.HIGHEST).astype(jnp.bfloat16)
    cells = jnp.einsum('ckzps,xpkq->cxzqs', as_float(along_z), as_float(inverse_x), precision=lax.Precision.HIGHEST).astype(jnp.bfloat16)
    chans, x_len, z_len = cells.shape[:3]
    flat = cells.reshape(chans * x_len * z_len, -1)
    return (jnp.dot(flat, plane.T, preferred_element_type=jnp.float32) * scale).reshape(chans, x_len, z_len, -1)

def mode_product(weight, modes, adjoint):
    real_w = as_float(weight[0])
    imag_w = as_float(weight[1])
    real_m = as_float(modes[:, :, :, 0, :])
    imag_m = as_float(modes[:, :, :, 1, :])
    high = lax.Precision.HIGHEST
    if adjoint:
        form = 'cosxz,oxzs->cxzs'
        real_out = jnp.einsum(form, real_w, real_m, precision=high) + jnp.einsum(form, imag_w, imag_m, precision=high)
        imag_out = jnp.einsum(form, real_w, imag_m, precision=high) - jnp.einsum(form, imag_w, real_m, precision=high)
    else:
        form = 'cosxz,cxzs->oxzs'
        real_out = jnp.einsum(form, real_w, real_m, precision=high) - jnp.einsum(form, imag_w, imag_m, precision=high)
        imag_out = jnp.einsum(form, real_w, imag_m, precision=high) + jnp.einsum(form, imag_w, real_m, precision=high)
    return jnp.stack([real_out, imag_out], 3).astype(jnp.bfloat16)

def weight_grad(field_modes, grad_modes, scale):
    real_v = as_float(field_modes[:, :, :, 0, :])
    imag_v = as_float(field_modes[:, :, :, 1, :])
    real_d = as_float(grad_modes[:, :, :, 0, :])
    imag_d = as_float(grad_modes[:, :, :, 1, :])
    form = 'cxzs,oxzs->cosxz'
    real_g = (jnp.einsum(form, real_v, real_d) + jnp.einsum(form, imag_v, imag_d)) * scale
    imag_g = (jnp.einsum(form, real_v, imag_d) - jnp.einsum(form, imag_v, real_d)) * scale
    stacked = jnp.stack([real_g, imag_g], 0)
    shape = stacked.shape
    return stacked.reshape(2, shape[1], shape[2], shape[3], shape[4] * shape[5])

def gelu_slope(pre):
    normal_cdf = 0.5 * (1.0 + lax.erf(pre * (1.0 / math.sqrt(2.0))))
    return normal_cdf + pre * jnp.exp(-0.5 * pre * pre) * (1.0 / math.sqrt(2.0 * math.pi))

def reference(field, cotangent, spec_weight, mix_weight):
    chans, x_len, z_len, plane_len = field.shape
    plane = plane_table(NY, NSTEP, MY, MT)
    forward_x = pair_table(mode_angles(x_len, MX, False), False)
    inverse_x = pair_table(mode_angles(x_len, MX, False), True)
    forward_z = pair_table(mode_angles(z_len, MZ, False), False)
    inverse_z = pair_table(mode_angles(z_len, MZ, False), True)
    count = x_len * z_len * plane_len
    scale = 1.0 / count
    weight = spec_weight.reshape(2, chans, chans, MY * MT, MX, MZ)
    field_modes = to_modes(field, plane, forward_x, forward_z)
    out_modes = mode_product(weight, field_modes, False)
    spectral = to_field(out_modes, plane, inverse_x, inverse_z, scale)
    flat_field = field.reshape(chans, -1)
    mixed = jnp.dot(mix_weight.T, flat_field, preferred_element_type=jnp.float32).reshape(field.shape)
    pre = spectral + mixed
    grad_pre = (cotangent.astype(jnp.float32) * gelu_slope(pre)).astype(jnp.bfloat16)
    grad_modes = to_modes(grad_pre, plane, forward_x, forward_z)
    spec_grad = weight_grad(field_modes, grad_modes, scale)
    back_modes = mode_product(weight, grad_modes, True)
    back = to_field(back_modes, plane, inverse_x, inverse_z, scale)
    flat_grad = grad_pre.reshape(chans, -1)
    local_back = jnp.dot(mix_weight, flat_grad, preferred_element_type=jnp.float32).reshape(field.shape)
    field_grad = (back + local_back).astype(jnp.bfloat16)
    mix_grad = jnp.dot(flat_field, flat_grad.T, preferred_element_type=jnp.float32) * (1.0 / math.sqrt(count))
    return (field_grad, spec_grad, mix_grad)
```

```python
import functools
import math

import jax
import jax.numpy as jnp
import ml_dtypes
import numpy as np
from jax import lax
from jax.experimental import pallas as pl
from jax.experimental.pallas import tpu as pltpu
from jax.sharding import PartitionSpec as P

MX = 24
MY = 24
MZ = 16
MT = 8
NY = 128
NSTEP = 16
LANES = 128
MIX_ROWS = 4
BF = jnp.bfloat16
F32 = jnp.float32
VMEM_LIMIT = 40 * 1024 * 1024


def mode_angles(length, count, one_sided):
    cells = np.arange(length)
    ranks = np.arange(count)
    freqs = ranks if one_sided else np.where(ranks < count // 2, ranks, ranks - count)
    wrapped = np.mod(cells[:, None] * freqs[None, :], length)
    return wrapped.astype(np.float32) * np.float32(2.0 * math.pi / length)


def rounded(values):
    return np.asarray(values).astype(np.float32).astype(ml_dtypes.bfloat16).astype(np.float32)


def pair_table(angles, conjugate):
    cosine = rounded(np.cos(angles.astype(np.float64)))
    sine = rounded(np.sin(angles.astype(np.float64)))
    if conjugate:
        rows = [np.stack([cosine, sine], -1), np.stack([-sine, cosine], -1)]
    else:
        rows = [np.stack([cosine, -sine], -1), np.stack([sine, cosine], -1)]
    return np.stack(rows, 1)


def plane_rows():
    y_angle = mode_angles(NY, MY, False)
    t_angle = mode_angles(NSTEP, MT, True)
    total = (y_angle.T[:, None, :, None] + t_angle.T[None, :, None, :]).astype(np.float32)
    total = total.reshape(MY * MT, NY * NSTEP).astype(np.float64)
    return np.concatenate([np.cos(total), -np.sin(total)], 0)


class Plan:
    def __init__(self, field_shape, weight_shape, x_parts, z_parts):
        self.chans, self.xl, self.zl, self.plane = field_shape
        self.xp, self.zp = x_parts, z_parts
        self.x_len, self.z_len = self.xl * x_parts, self.zl * z_parts
        self.half = self.chans // 2
        self.s = weight_shape[3]
        self.modes = weight_shape[4]
        self.kxl = self.modes // MZ
        self.ms = self.s * x_parts
        self.xz = self.xl * self.zl
        self.rows = self.half * self.xz
        self.rows_pad = -(-self.rows // LANES) * LANES
        self.group = LANES // self.xz
        self.pairs = self.rows_pad // LANES
        self.width = self.xl * 2 * MZ
        self.blocks = self.half // 2
        self.used = self.blocks * self.s
        self.chunk = -(-(self.used + MIX_ROWS) // 16) * 16
        self.count = self.x_len * self.z_len * self.plane
        self.scale = 1.0 / self.count
        assert z_parts == 2 and 2 * self.width == LANES and self.group * self.xz == LANES
        assert self.zl == MZ

    def tables(self):
        bf = lambda t: np.ascontiguousarray(t).astype(ml_dtypes.bfloat16)
        g = self.group * self.xl
        eye = np.eye(g, dtype=np.float32)
        zf = pair_table(mode_angles(self.z_len, MZ, False), False)
        zf = zf.reshape(2, self.zl, 2, MZ, 2)
        zf = np.einsum("hzplq,ab->hpazbql", zf, eye).reshape(2, 2 * LANES, 2 * LANES)
        z_forward = np.stack([np.concatenate([zf[0], zf[1]], 0), np.concatenate([zf[1], zf[0]], 0)])
        zi = pair_table(mode_angles(self.z_len, MZ, False), True)
        zi = zi.reshape(2, self.zl, 2, MZ, 2)
        zi = np.einsum("hzplq,ab->hqazbpl", zi, eye).reshape(2, 2 * LANES, 2 * LANES)
        z_inverse = np.stack([np.concatenate([zi[1], zi[0]], 0), np.concatenate([zi[0], zi[1]], 0)])
        eye = np.eye(MZ, dtype=np.float32)
        xf = pair_table(mode_angles(self.x_len, MX, False), False)
        xf = xf.reshape(self.x_len, 2, 2, self.kxl, 2)
        x_forward = np.einsum("xpjkr,ab->jrxpakb", xf, eye)
        x_forward = x_forward.reshape(2, 2, self.xp * self.width, self.modes)
        xi = pair_table(mode_angles(self.x_len, MX, False), True)
        xi = xi.reshape(self.x_len, 2, 2, self.kxl, 2)
        x_inverse = np.einsum("xrjkq,ab->jrkaxqb", xi, eye)
        x_inverse = x_inverse.reshape(2, 2, self.modes, self.xp * self.width)
        owner = np.repeat(np.eye(self.chans, dtype=np.float32), self.xz, axis=0)
        return dict(
            plane=bf(plane_rows()),
            z_forward=bf(z_forward),
            z_inverse=bf(z_inverse),
            x_forward=bf(x_forward),
            x_inverse=bf(x_inverse),
            owner=bf(owner),
        )


def params(**kw):
    return pltpu.CompilerParams(vmem_limit_bytes=VMEM_LIMIT, **kw)


def cost(flops, nbytes):
    return pl.CostEstimate(flops=int(flops), bytes_accessed=int(nbytes), transcendentals=0)


def shape(dims, kind=BF):
    return jax.ShapeDtypeStruct(tuple(dims), kind)


def full(dims):
    return pl.BlockSpec(tuple(dims), lambda *_: (0,) * len(dims))


def dot(a, b):
    return lax.dot_general(a, b, (((1,), (0,)), ((), ())), preferred_element_type=F32)


def dot_t(a, b):
    return lax.dot_general(a, b, (((1,), (1,)), ((), ())), preferred_element_type=F32)


def plane_forward(plan, which, field, plane):
    tiles = 4
    width = plan.plane // tiles

    def kernel(_, field_ref, plane_ref, out_ref, acc_ref):
        step = pl.program_id(0)
        value = dot_t(plane_ref[...], field_ref[0])

        @pl.when(step == 0)
        def _():
            acc_ref[...] = value

        @pl.when(step > 0)
        def _():
            acc_ref[...] += value

        @pl.when(step == tiles - 1)
        def _():
            if plan.rows_pad > plan.rows:
                pad = plan.rows_pad - plan.rows
                out_ref[:, plan.rows :] = jnp.zeros((2 * plan.ms, pad), BF)
            out_ref[:, : plan.rows] = acc_ref[...].astype(BF)

    return pl.pallas_call(
        kernel,
        grid_spec=pltpu.PrefetchScalarGridSpec(
            num_scalar_prefetch=1,
            grid=(tiles,),
            in_specs=[
                pl.BlockSpec((1, plan.rows, width), lambda t, h: (h[0], 0, t)),
                pl.BlockSpec((2 * plan.ms, width), lambda t, h: (0, t)),
            ],
            out_specs=full((2 * plan.ms, plan.rows_pad)),
            scratch_shapes=[pltpu.VMEM((2 * plan.ms, plan.rows), F32)],
        ),
        out_shape=shape((2 * plan.ms, plan.rows_pad)),
        compiler_params=params(),
        cost_estimate=cost(4 * plan.ms * plan.rows * plan.plane, 3.2e6),
        name="plane_forward",
    )(which, field.reshape(2, plan.rows, plan.plane), plane)


def z_forward(plan, me, own, got, table):
    def kernel(_, own_ref, got_ref, table_ref, out_ref, lines, pieces):
        ms = plan.ms
        for g in range(plan.pairs):
            at = slice(g * LANES, (g + 1) * LANES)
            parts = [own_ref[:ms, at], own_ref[ms:, at], got_ref[:ms, at], got_ref[ms:, at]]
            value = dot(jnp.concatenate(parts, 1), table_ref[0])
            for b in (0, 1):
                if 2 * g + b < plan.blocks:
                    lines[2 * g + b] = value[:, b * LANES : (b + 1) * LANES]
        pad = plan.chunk - plan.used
        for i in range(plan.xp):
            for b in range(plan.blocks):
                pieces[i, b * plan.s : (b + 1) * plan.s, :] = lines[b, i * plan.s : (i + 1) * plan.s, :]
            pieces[i, plan.used :, :] = jnp.zeros((pad, LANES), F32)
            out_ref[i] = pieces[i].astype(BF)

    side = (2 * plan.ms, plan.rows_pad)
    return pl.pallas_call(
        kernel,
        grid_spec=pltpu.PrefetchScalarGridSpec(
            num_scalar_prefetch=1,
            grid=(1,),
            in_specs=[
                full(side),
                full(side),
                pl.BlockSpec((1, 4 * LANES, 2 * LANES), lambda t, j: (j[0], 0, 0)),
            ],
            out_specs=full((plan.xp, plan.chunk, LANES)),
            scratch_shapes=[
                pltpu.VMEM((plan.blocks, plan.ms, LANES), F32),
                pltpu.VMEM((plan.xp, plan.chunk, LANES), F32),
            ],
        ),
        out_shape=shape((plan.xp, plan.chunk, LANES)),
        compiler_params=params(),
        cost_estimate=cost(3e8, 1e6),
        name="z_forward",
    )(me, own, got, table)


def x_forward(plan, me, chunks, table):
    def kernel(me_ref, in_ref, table_ref, send_ref, keep_ref, lhs, lines):
        w = plan.width
        for i in range(0, plan.xp, 2):
            first, second = in_ref[i], in_ref[i + 1]
            at = slice(i * w, (i + 2) * w)
            lhs[: plan.chunk, at] = jnp.concatenate([first[:, :w], second[:, :w]], 1)
            lhs[plan.chunk :, at] = jnp.concatenate([first[:, w:], second[:, w:]], 1)
        me = me_ref[0]
        for slot, half, out_ref in ((0, 1 - me, send_ref), (1, me, keep_ref)):
            for r in (0, 1):
                lines[slot, r] = dot(lhs[...], table_ref[half, r])
                for c in range(plan.half):
                    start = (c % 2) * plan.chunk + (c // 2) * plan.s
                    out_ref[c, r] = lines[slot, r, start : start + plan.s, :].astype(BF)

    out = (plan.half, 2, plan.s, plan.modes)
    return pl.pallas_call(
        kernel,
        grid_spec=pltpu.PrefetchScalarGridSpec(
            num_scalar_prefetch=1,
            grid=(1,),
            in_specs=[full((plan.xp, plan.chunk, LANES)), full(table.shape)],
            out_specs=[full(out), full(out)],
            scratch_shapes=[
                pltpu.VMEM((2 * plan.chunk, plan.xp * plan.width), BF),
                pltpu.VMEM((2, 2, 2 * plan.chunk, plan.modes), F32),
            ],
        ),
        out_shape=[shape(out), shape(out)],
        compiler_params=params(),
        cost_estimate=cost(3e8, 3e6),
        name="x_forward",
    )(me, chunks, table)


def mode_product(plan, me, which, weight, own, got, adjoint):
    block = 2
    steps = plan.half // block

    def kernel(me_ref, _, weight_ref, own_ref, got_ref, out_ref, held):
        me = me_ref[0]

        @pl.when(pl.program_id(0) == 0)
        def _():
            held[me] = own_ref[...].astype(F32)
            held[1 - me] = got_ref[...].astype(F32)

        for k in range(block):
            real = jnp.zeros((plan.s, plan.modes), F32)
            imag = jnp.zeros((plan.s, plan.modes), F32)
            for c in range(plan.chans):
                pos = (k, c) if adjoint else (c, k)
                wr = weight_ref[0, pos[0], pos[1]].astype(F32)
                wi = weight_ref[1, pos[0], pos[1]].astype(F32)
                mr = held[c // plan.half, c % plan.half, 0]
                mi = held[c // plan.half, c % plan.half, 1]
                if adjoint:
                    real += wr * mr + wi * mi
                    imag += wr * mi - wi * mr
                else:
                    real += wr * mr - wi * mi
                    imag += wr * mi + wi * mr
            out_ref[k, 0] = real.astype(BF)
            out_ref[k, 1] = imag.astype(BF)

    side = (plan.half, 2, plan.s, plan.modes)
    if adjoint:
        w_block = (2, block, plan.chans, plan.s, plan.modes)
        w_map = lambda t, j, h: (0, h[0] * steps + t, 0, 0, 0)
    else:
        w_block = (2, plan.chans, block, plan.s, plan.modes)
        w_map = lambda t, j, h: (0, 0, h[0] * steps + t, 0, 0)
    return pl.pallas_call(
        kernel,
        grid_spec=pltpu.PrefetchScalarGridSpec(
            num_scalar_prefetch=2,
            grid=(steps,),
            in_specs=[pl.BlockSpec(w_block, w_map), full(side), full(side)],
            out_specs=pl.BlockSpec((block, 2, plan.s, plan.modes), lambda t, j, h: (t, 0, 0, 0)),
            scratch_shapes=[pltpu.VMEM((2,) + side, F32)],
        ),
        out_shape=shape(side),
        compiler_params=params(),
        cost_estimate=cost(4e9, 4e6),
        name="mode_product",
    )(me, which, weight, own, got)


def x_inverse(plan, me, own, got, table, mix):
    carry = mix is not None

    def kernel(me_ref, own_ref, got_ref, table_ref, *rest):
        mix_ref = rest[0] if carry else None
        out_ref, lhs, spare = rest[1:] if carry else rest
        me = me_ref[0]
        pad = plan.chunk - plan.used
        for slot, in_ref in ((0, own_ref), (1, got_ref)):
            for r in (0, 1):
                for c in range(plan.half):
                    start = (c % 2) * plan.chunk + (c // 2) * plan.s
                    lhs[slot, r, start : start + plan.s, :] = in_ref[c, r].astype(F32)
                for c in (0, 1):
                    start = c * plan.chunk + plan.used
                    lhs[slot, r, start : start + pad, :] = jnp.zeros((pad, plan.modes), F32)
        value = None
        for slot, half in ((0, me), (1, 1 - me)):
            for r in (0, 1):
                term = dot(lhs[slot, r].astype(BF), table_ref[half, r])
                value = term if value is None else value + term
        w = plan.width
        if carry:
            spare[...] = jnp.zeros((plan.chunk, LANES), F32)
            spare[plan.used : plan.used + MIX_ROWS, :] = mix_ref[...]
        for i in range(plan.xp):
            first = value[: plan.chunk, i * w : (i + 1) * w]
            second = value[plan.chunk :, i * w : (i + 1) * w]
            piece = jnp.concatenate([first, second], 1)
            if carry:
                piece = piece + spare[...]
            out_ref[i] = piece.astype(BF)

    side = (plan.half, 2, plan.s, plan.modes)
    extra = [full((MIX_ROWS, LANES))] if carry else []
    return pl.pallas_call(
        kernel,
        grid_spec=pltpu.PrefetchScalarGridSpec(
            num_scalar_prefetch=1,
            grid=(1,),
            in_specs=[full(side), full(side), full(table.shape)] + extra,
            out_specs=full((plan.xp, plan.chunk, LANES)),
            scratch_shapes=[
                pltpu.VMEM((2, 2, 2 * plan.chunk, plan.modes), F32),
                pltpu.VMEM((plan.chunk, LANES), F32),
            ],
        ),
        out_shape=shape((plan.xp, plan.chunk, LANES)),
        compiler_params=params(),
        cost_estimate=cost(3e8, 3e6),
        name="x_inverse",
    )(me, own, got, table, *([mix] if carry else []))


def z_inverse(plan, me, chunks, table, carry):
    def kernel(_, in_ref, table_ref, send_ref, keep_ref, *rest):
        mix_ref = rest[0] if carry else None
        lines, pieces = rest[-2:]
        s, ms = plan.s, plan.ms
        for i in range(plan.xp):
            pieces[i] = in_ref[i].astype(F32)
            for b in range(plan.blocks):
                lines[b, i * s : (i + 1) * s, :] = pieces[i, b * s : (b + 1) * s, :]
        for g in range(plan.pairs):
            first = lines[2 * g].astype(BF)
            if 2 * g + 1 < plan.blocks:
                second = lines[2 * g + 1].astype(BF)
            else:
                second = jnp.zeros((ms, LANES), BF)
            value = dot_t(table_ref[0], jnp.concatenate([first, second], 1))
            rows = min(LANES, plan.rows - g * LANES)
            for slot, out_ref in ((0, send_ref), (1, keep_ref)):
                for p in (0, 1):
                    start = (2 * slot + p) * LANES
                    out_ref[p, g * LANES : g * LANES + rows, :] = value[start : start + rows].astype(BF)
        if carry:
            total = pieces[0, plan.used : plan.used + MIX_ROWS, :]
            for i in range(1, plan.xp):
                total = total + pieces[i, plan.used : plan.used + MIX_ROWS, :]
            mix_ref[...] = total

    out = (2, plan.rows, plan.ms)
    outs = [out, out]
    out_shape = [shape(out), shape(out)]
    if carry:
        outs.append((MIX_ROWS, LANES))
        out_shape.append(shape((MIX_ROWS, LANES), F32))
    return pl.pallas_call(
        kernel,
        grid_spec=pltpu.PrefetchScalarGridSpec(
            num_scalar_prefetch=1,
            grid=(1,),
            in_specs=[
                full((plan.xp, plan.chunk, LANES)),
                pl.BlockSpec((1, 4 * LANES, 2 * LANES), lambda t, j: (j[0], 0, 0)),
            ],
            out_specs=[full(o) for o in outs],
            scratch_shapes=[
                pltpu.VMEM((plan.blocks, plan.ms, LANES), F32),
                pltpu.VMEM((plan.xp, plan.chunk, LANES), F32),
            ],
        ),
        out_shape=out_shape,
        compiler_params=params(),
        cost_estimate=cost(3e8, 1e6),
        name="z_inverse",
    )(me, chunks, table)


def mix_blocks(plan, mix, owner):
    cells = 2 * plan.rows

    def kernel(mix_ref, back_ref, owner_ref, owner_t_ref, out_ref):
        row = lax.broadcasted_iota(jnp.int32, (plan.rows, cells), 0) % plan.xz
        col = lax.broadcasted_iota(jnp.int32, (plan.rows, cells), 1) % plan.xz
        same = row == col
        for d, ref in ((0, mix_ref), (1, back_ref)):
            for h in (0, 1):
                spread = dot(owner_ref[h * plan.rows : (h + 1) * plan.rows, :], ref[...]).astype(BF)
                wide = dot(spread, owner_t_ref[...])
                out_ref[d, h] = jnp.where(same, wide, 0.0).astype(BF)

    return pl.pallas_call(
        kernel,
        out_shape=shape((2, 2, plan.rows, cells)),
        compiler_params=params(),
        cost_estimate=cost(4e7, 2e6),
        name="mix_blocks",
    )(mix.T, mix, owner, owner.T)


def gelu_slope(pre):
    size = jnp.abs(pre)
    bell = jnp.exp(pre * pre * -0.5)
    t = 1.0 / (1.0 + size * (0.3275911 / math.sqrt(2.0)))
    poly = 0.5 * 1.061405429
    for coef in (-1.453152027, 1.421413741, -0.284496736, 0.254829592):
        poly = poly * t + 0.5 * coef
    tail = poly * t * bell
    cdf = jnp.where(pre < 0.0, tail, 1.0 - tail)
    return cdf + pre * bell * (1.0 / math.sqrt(2.0 * math.pi))


def cells_forward(plan, me, own, got, plane, mixing, field, cotangent):
    tiles = 4
    width = plan.plane // tiles
    stripe = 32

    def kernel(me_ref, own_ref, got_ref, plane_ref, mix_ref, field_ref, cot_ref, grad_ref, send_ref, keep_ref, pre, acc):
        me = me_ref[0]
        step = pl.program_id(0)
        ms = plan.ms
        for slot, half, in_ref in ((0, me, own_ref), (1, 1 - me, got_ref)):
            spectral = dot(in_ref[0], plane_ref[:ms]) + dot(in_ref[1], plane_ref[ms:])
            mixed = dot(mix_ref[0, half], field_ref[...])
            pre[slot] = spectral * plan.scale + mixed
            for r in range(0, plan.rows, stripe):
                at = slice(r, r + stripe)
                slope = gelu_slope(pre[slot, at, :])
                grad_ref[half, at, :] = (cot_ref[half, at, :].astype(F32) * slope).astype(BF)
            value = dot_t(plane_ref[...], grad_ref[half])

            @pl.when(step == 0)
            def _():
                acc[slot] = value

            @pl.when(step > 0)
            def _():
                acc[slot] += value

        @pl.when(step == tiles - 1)
        def _():
            for slot, out_ref in ((0, keep_ref), (1, send_ref)):
                if plan.rows_pad > plan.rows:
                    pad = plan.rows_pad - plan.rows
                    out_ref[:, plan.rows :] = jnp.zeros((2 * ms, pad), BF)
                out_ref[:, : plan.rows] = acc[slot].astype(BF)

    side = (2, plan.rows, plan.ms)
    out = (2 * plan.ms, plan.rows_pad)
    cells = (2, plan.rows, plan.plane)
    tile = pl.BlockSpec((2, plan.rows, width), lambda t, j: (0, 0, t))
    return pl.pallas_call(
        kernel,
        grid_spec=pltpu.PrefetchScalarGridSpec(
            num_scalar_prefetch=1,
            grid=(tiles,),
            in_specs=[
                full(side),
                full(side),
                pl.BlockSpec((2 * plan.ms, width), lambda t, j: (0, t)),
                pl.BlockSpec((1, 2, plan.rows, 2 * plan.rows), lambda t, j: (0, 0, 0, 0)),
                pl.BlockSpec((2 * plan.rows, width), lambda t, j: (0, t)),
                tile,
            ],
            out_specs=[tile, full(out), full(out)],
            scratch_shapes=[
                pltpu.VMEM((2, plan.rows, width), F32),
                pltpu.VMEM((2, 2 * plan.ms, plan.rows), F32),
            ],
        ),
        out_shape=[shape(cells), shape(out), shape(out)],
        compiler_params=params(),
        cost_estimate=cost(6e9, 1e7),
        name="cells_forward",
    )(me, own, got, plane, mixing, field.reshape(2 * plan.rows, plan.plane), cotangent.reshape(cells))


def cells_back(plan, me, own, got, plane, mixing, grad):
    tiles = 4
    width = plan.plane // tiles

    def kernel(me_ref, own_ref, got_ref, plane_ref, mix_ref, grad_ref, out_ref):
        me = me_ref[0]
        ms = plan.ms
        for half, in_ref in ((me, own_ref), (1 - me, got_ref)):
            spectral = dot(in_ref[0], plane_ref[:ms]) + dot(in_ref[1], plane_ref[ms:])
            mixed = dot(mix_ref[0, half], grad_ref[...])
            out_ref[half] = (spectral * plan.scale + mixed).astype(BF)

    side = (2, plan.rows, plan.ms)
    cells = (2, plan.rows, plan.plane)
    return pl.pallas_call(
        kernel,
        grid_spec=pltpu.PrefetchScalarGridSpec(
            num_scalar_prefetch=1,
            grid=(tiles,),
            in_specs=[
                full(side),
                full(side),
                pl.BlockSpec((2 * plan.ms, width), lambda t, j: (0, t)),
                pl.BlockSpec((1, 2, plan.rows, 2 * plan.rows), lambda t, j: (1, 0, 0, 0)),
                pl.BlockSpec((2 * plan.rows, width), lambda t, j: (0, t)),
            ],
            out_specs=pl.BlockSpec((2, plan.rows, width), lambda t, j: (0, 0, t)),
        ),
        out_shape=shape(cells),
        compiler_params=params(),
        cost_estimate=cost(4e9, 8e6),
        name="cells_back",
    )(me, own, got, plane, mixing, grad.reshape(2 * plan.rows, plan.plane))


def pack_tables(plan):
    per_row = plan.chans // MIX_ROWS
    lane = LANES // per_row
    assert per_row * MIX_ROWS == plan.chans and lane >= plan.chans
    pick = np.zeros((per_row, MIX_ROWS, plan.chans), np.float32)
    place = np.zeros((per_row, 2 * plan.rows, LANES), np.float32)
    for k in range(per_row):
        for r in range(MIX_ROWS):
            pick[k, r, r * per_row + k] = 1.0
        for cell in range(2 * plan.rows):
            place[k, cell, k * lane + cell // plan.xz] = 1.0
    return pick, place.astype(ml_dtypes.bfloat16)


def mix_partial(plan, field, grad):
    tiles = 4
    width = plan.plane // tiles
    cells = 2 * plan.rows
    pick, place = pack_tables(plan)
    factor = 1.0 / math.sqrt(plan.count)

    def kernel(field_ref, grad_ref, pick_ref, place_ref, out_ref, acc):
        step = pl.program_id(0)
        value = dot_t(field_ref[...], grad_ref[...])

        @pl.when(step == 0)
        def _():
            acc[...] = value

        @pl.when(step > 0)
        def _():
            acc[...] += value

        @pl.when(step == tiles - 1)
        def _():
            row = lax.broadcasted_iota(jnp.int32, (plan.xz, cells), 0)
            col = lax.broadcasted_iota(jnp.int32, (plan.xz, cells), 1) % plan.xz
            same = row == col
            lines = []
            for c in range(plan.chans):
                part = jnp.where(same, acc[c * plan.xz : (c + 1) * plan.xz, :], 0.0)
                lines.append(jnp.sum(part, 0, keepdims=True))
            sums = jnp.concatenate(lines, 0) * factor
            high = sums.astype(BF)
            low = (sums - high.astype(F32)).astype(BF)
            total = jnp.zeros((MIX_ROWS, LANES), F32)
            for k in range(plan.chans // MIX_ROWS):
                spread = dot(high, place_ref[k]) + dot(low, place_ref[k])
                total += lax.dot_general(
                    pick_ref[k], spread, (((1,), (0,)), ((), ())),
                    precision=lax.Precision.HIGHEST, preferred_element_type=F32,
                )
            out_ref[...] = total

    tile = pl.BlockSpec((cells, width), lambda t: (0, t))
    return pl.pallas_call(
        kernel,
        grid=(tiles,),
        in_specs=[tile, tile, full(pick.shape), full(place.shape)],
        out_specs=full((MIX_ROWS, LANES)),
        scratch_shapes=[pltpu.VMEM((cells, cells), F32)],
        out_shape=shape((MIX_ROWS, LANES), F32),
        compiler_params=params(),
        cost_estimate=cost(4e9, 6e6),
        name="mix_partial",
    )(field.reshape(cells, plan.plane), grad.reshape(cells, plan.plane), pick, place)


def weight_grad(plan, me, field_own, field_got, grad_own, grad_got):
    chans, half = plan.chans, plan.half

    def kernel(me_ref, fo_ref, fg_ref, go_ref, gg_ref, out_ref, held, line):
        me = me_ref[0]
        step = pl.program_id(0)

        @pl.when(step == 0)
        def _():
            held[me] = go_ref[...].astype(F32)
            held[1 - me] = gg_ref[...].astype(F32)

        @pl.when(step < half)
        def _():
            line[...] = fo_ref[step % half].astype(F32) * plan.scale

        @pl.when(step >= half)
        def _():
            line[...] = fg_ref[step % half].astype(F32) * plan.scale

        vr, vi = line[0], line[1]
        for o in range(chans):
            dr = held[o // half, o % half, 0]
            di = held[o // half, o % half, 1]
            out_ref[0, 0, o] = vr * dr + vi * di
            out_ref[1, 0, o] = vr * di - vi * dr

    side = (half, 2, plan.s, plan.modes)
    return pl.pallas_call(
        kernel,
        grid_spec=pltpu.PrefetchScalarGridSpec(
            num_scalar_prefetch=1,
            grid=(chans,),
            in_specs=[full(side)] * 4,
            out_specs=pl.BlockSpec(
                (2, 1, chans, plan.s, plan.modes), lambda t, j: (0, (j[0] * half + t) % chans, 0, 0, 0)
            ),
            scratch_shapes=[pltpu.VMEM((2,) + side, F32), pltpu.VMEM(side[1:], F32)],
        ),
        out_shape=shape((2, chans, chans, plan.s, plan.modes), F32),
        compiler_params=params(),
        cost_estimate=cost(8e9, 1.3e7),
        name="weight_grad",
    )(me, field_own, field_got, grad_own, grad_got)


def local(x_parts, z_parts, field, cotangent, spec_weight, mix_weight):
    plan = Plan(field.shape, spec_weight.shape, x_parts, z_parts)
    const = {name: jnp.asarray(value) for name, value in plan.tables().items()}
    core = lax.axis_index("gz").astype(jnp.int32)
    me = core.reshape(1)
    other = (1 - core).reshape(1)
    plane = const["plane"]

    def swap(value):
        return lax.ppermute(value, "gz", [(0, 1), (1, 0)])

    def spread(chunks):
        return lax.all_to_all(chunks, "gx", split_axis=0, concat_axis=0, tiled=True)

    def to_modes(keep, got):
        chunks = spread(z_forward(plan, me, keep, got, const["z_forward"]))
        send, own = x_forward(plan, me, chunks, const["x_forward"])
        return own, swap(send)

    def product(own, got, adjoint):
        send = mode_product(plan, me, other, spec_weight, own, got, adjoint)
        keep = mode_product(plan, me, me, spec_weight, own, got, adjoint)
        return keep, swap(send)

    def to_cells(keep, got, mix):
        chunks = spread(x_inverse(plan, me, keep, got, const["x_inverse"], mix))
        outs = z_inverse(plan, me, chunks, const["z_inverse"], mix is not None)
        return outs[1], swap(outs[0]), outs[2:]

    mixing = mix_blocks(plan, mix_weight, const["owner"])
    send = plane_forward(plan, other, field, plane)
    keep = plane_forward(plan, me, field, plane)
    field_own, field_got = to_modes(keep, swap(send))
    keep, got = product(field_own, field_got, False)
    keep, got, _ = to_cells(keep, got, None)
    grad, send, keep = cells_forward(plan, me, keep, got, plane, mixing, field, cotangent)
    grad_own, grad_got = to_modes(keep, swap(send))
    partial_mix = mix_partial(plan, field, grad)
    partial_mix = partial_mix + swap(partial_mix)
    keep, got = product(grad_own, grad_got, True)
    spec_grad = weight_grad(plan, me, field_own, field_got, grad_own, grad_got)
    keep, got, mix = to_cells(keep, got, partial_mix)
    field_grad = cells_back(plan, me, keep, got, plane, mixing, grad).reshape(field.shape)
    per_row = plan.chans // MIX_ROWS
    lane = LANES // per_row
    mix_grad = mix[0][:, : per_row * lane].reshape(MIX_ROWS, per_row, lane)[:, :, : plan.chans]
    return (field_grad, spec_grad, mix_grad.reshape(plan.chans, plan.chans))


def solution(mesh):
    placed = (
        P(None, ("grp", "gx"), "gz", None),
        P(None, ("grp", "gx"), "gz", None),
        P(None, None, None, "gx", "gz"),
        P(),
    )
    return jax.shard_map(
        functools.partial(local, mesh.shape["gx"], mesh.shape["gz"]),
        mesh=mesh,
        in_specs=placed,
        out_specs=(
            P(None, ("grp", "gx"), "gz", None),
            P("grp", None, None, "gx", "gz"),
            P("grp", None),
        ),
        check_vma=False,
    )
```

```python
import functools
import math

import jax
import jax.numpy as jnp
import ml_dtypes
import numpy as np
from jax import lax
from jax.experimental import pallas as pl
from jax.experimental.layout import Layout, with_layout_constraint
from jax.experimental.pallas import tpu as pltpu
from jax.sharding import PartitionSpec as P

MX = 24
MY = 24
MZ = 16
MT = 8
NY = 128
NSTEP = 16
LANES = 128
MIX_ROWS = 4
BF = jnp.bfloat16
F32 = jnp.float32
VMEM_LIMIT = 18 * 1024 * 1024


def mode_angles(length, count, one_sided):
    cells = np.arange(length)
    ranks = np.arange(count)
    freqs = ranks if one_sided else np.where(ranks < count // 2, ranks, ranks - count)
    wrapped = np.mod(cells[:, None] * freqs[None, :], length)
    return wrapped.astype(np.float32) * np.float32(2.0 * math.pi / length)


def rounded(values):
    return np.asarray(values).astype(np.float32).astype(ml_dtypes.bfloat16).astype(np.float32)


def pair_table(angles, conjugate):
    cosine = rounded(np.cos(angles.astype(np.float64)))
    sine = rounded(np.sin(angles.astype(np.float64)))
    if conjugate:
        rows = [np.stack([cosine, sine], -1), np.stack([-sine, cosine], -1)]
    else:
        rows = [np.stack([cosine, -sine], -1), np.stack([sine, cosine], -1)]
    return np.stack(rows, 1)


def plane_rows():
    y_angle = mode_angles(NY, MY, False)
    t_angle = mode_angles(NSTEP, MT, True)
    total = (y_angle.T[:, None, :, None] + t_angle.T[None, :, None, :]).astype(np.float32)
    total = total.reshape(MY * MT, NY * NSTEP).astype(np.float64)
    return np.concatenate([np.cos(total), -np.sin(total)], 0)


class Plan:
    def __init__(self, field_shape, weight_shape, x_parts, z_parts):
        self.chans, self.xl, self.zl, self.plane = field_shape
        self.xp, self.zp = x_parts, z_parts
        self.x_len, self.z_len = self.xl * x_parts, self.zl * z_parts
        self.half = self.chans // 2
        self.s = weight_shape[3]
        self.modes = weight_shape[4]
        self.kxl = self.modes // MZ
        self.ms = self.s * x_parts
        self.xz = self.xl * self.zl
        self.rows = self.half * self.xz
        self.rows_pad = -(-self.rows // LANES) * LANES
        self.group = LANES // self.xz
        self.pairs = self.rows_pad // LANES
        self.width = self.xl * 2 * MZ
        self.blocks = self.half // 2
        self.used = self.blocks * self.s
        self.chunk = -(-(self.used + MIX_ROWS) // 16) * 16
        self.count = self.x_len * self.z_len * self.plane
        self.scale = 1.0 / self.count
        assert z_parts == 2 and 2 * self.width == LANES and self.group * self.xz == LANES
        assert self.zl == MZ

    def tables(self):
        bf = lambda t: np.ascontiguousarray(t).astype(ml_dtypes.bfloat16)
        g = self.group * self.xl
        eye = np.eye(g, dtype=np.float32)
        zf = pair_table(mode_angles(self.z_len, MZ, False), False)
        zf = zf.reshape(2, self.zl, 2, MZ, 2)
        zf = np.einsum("hzplq,ab->hpazbql", zf, eye).reshape(2, 2 * LANES, 2 * LANES)
        z_forward = np.stack([np.concatenate([zf[0], zf[1]], 0), np.concatenate([zf[1], zf[0]], 0)])
        zi = pair_table(mode_angles(self.z_len, MZ, False), True)
        zi = zi.reshape(2, self.zl, 2, MZ, 2)
        zi = np.einsum("hzplq,ab->hqazbpl", zi, eye).reshape(2, 2 * LANES, 2 * LANES)
        z_inverse = np.stack([np.concatenate([zi[1], zi[0]], 0), np.concatenate([zi[0], zi[1]], 0)])
        eye = np.eye(MZ, dtype=np.float32)
        xf = pair_table(mode_angles(self.x_len, MX, False), False)
        xf = xf.reshape(self.x_len, 2, 2, self.kxl, 2)
        x_forward = np.einsum("xpjkr,ab->jrxpakb", xf, eye)
        x_forward = x_forward.reshape(2, 2, self.xp * self.width, self.modes)
        xi = pair_table(mode_angles(self.x_len, MX, False), True)
        xi = xi.reshape(self.x_len, 2, 2, self.kxl, 2)
        x_inverse = np.einsum("xrjkq,ab->jrkaxqb", xi, eye)
        x_inverse = x_inverse.reshape(2, 2, self.modes, self.xp * self.width)
        owner = np.repeat(np.eye(self.chans, dtype=np.float32), self.xz, axis=0)
        return dict(
            plane=bf(plane_rows()),
            z_forward=bf(z_forward),
            z_inverse=bf(z_inverse),
            x_forward=bf(x_forward),
            x_inverse=bf(x_inverse),
            owner=bf(owner),
        )


def params(**kw):
    return pltpu.CompilerParams(vmem_limit_bytes=VMEM_LIMIT, **kw)


def cost(flops, nbytes):
    return pl.CostEstimate(flops=int(flops), bytes_accessed=int(nbytes), transcendentals=0)


def hbm(value):
    return pltpu.with_memory_space_constraint(value, pltpu.HBM)


def vmem(value):
    return pltpu.with_memory_space_constraint(value, pltpu.VMEM)


WHOLE = pl.BlockSpec(memory_space=pltpu.VMEM)
SCALAR = pl.BlockSpec(memory_space=pltpu.SMEM)
ANYWHERE = pl.BlockSpec(memory_space=pl.ANY)


def shape(dims, kind=BF):
    return jax.ShapeDtypeStruct(tuple(dims), kind)


def full(dims):
    return pl.BlockSpec(tuple(dims), lambda *_: (0,) * len(dims))


def dot(a, b):
    return lax.dot_general(a, b, (((1,), (0,)), ((), ())), preferred_element_type=F32)


def dot_t(a, b):
    return lax.dot_general(a, b, (((1,), (1,)), ((), ())), preferred_element_type=F32)


def pad_lanes(plan, out_ref):
    if plan.rows_pad > plan.rows:
        pad = plan.rows_pad - plan.rows
        out_ref[:, plan.rows :] = jnp.zeros((2 * plan.ms, pad), BF)


def half_rows(plan, half):
    return pl.ds(pl.multiple_of(2 * plan.ms + half * plan.rows, math.gcd(2 * plan.ms, plan.rows)), plan.rows)


def load_forward(plan, me, field, plane):
    tiles = 4
    width = plan.plane // tiles
    ms2 = 2 * plan.ms

    def kernel(me_ref, field_ref, plane_ref, stack_ref, out_ref, acc, sems):
        me = me_ref[0]
        copies = []
        for k in range(tiles):
            at = slice(k * width, (k + 1) * width)
            copies.append(
                (
                    pltpu.make_async_copy(plane_ref.at[:, at], stack_ref.at[:ms2, at], sems.at[0, k]),
                    pltpu.make_async_copy(
                        field_ref.at[1 - me, :, at], stack_ref.at[half_rows(plan, 1 - me), at], sems.at[1, k]
                    ),
                    pltpu.make_async_copy(
                        field_ref.at[me, :, at], stack_ref.at[half_rows(plan, me), at], sems.at[2, k]
                    ),
                )
            )
        for group in copies:
            group[0].start()
            group[1].start()
        for group in copies:
            group[2].start()
        for k, group in enumerate(copies):
            at = slice(k * width, (k + 1) * width)
            group[0].wait()
            group[1].wait()
            value = dot_t(stack_ref[:ms2, at], stack_ref[half_rows(plan, 1 - me), at])
            if k == 0:
                acc[...] = value
            else:
                acc[...] += value
        pad_lanes(plan, out_ref)
        out_ref[:, : plan.rows] = acc[...].astype(BF)
        for group in copies:
            group[2].wait()

    return pl.pallas_call(
        kernel,
        in_specs=[SCALAR, ANYWHERE, ANYWHERE],
        out_specs=[WHOLE, WHOLE],
        out_shape=[pltpu.VMEM((ms2 + 2 * plan.rows, plan.plane), BF), shape((ms2, plan.rows_pad))],
        scratch_shapes=[pltpu.VMEM((ms2, plan.rows), F32), pltpu.SemaphoreType.DMA((3, tiles))],
        compiler_params=params(),
        cost_estimate=cost(4 * plan.ms * plan.rows * plan.plane, 5e6),
        name="load_forward",
    )(me, hbm(field.reshape(2, plan.rows, plan.plane)), hbm(plane))


def plane_forward(plan, me, stack):
    ms2 = 2 * plan.ms

    def kernel(me_ref, stack_ref, out_ref):
        value = dot_t(stack_ref[:ms2, :], stack_ref[half_rows(plan, me_ref[0]), :])
        pad_lanes(plan, out_ref)
        out_ref[:, : plan.rows] = value.astype(BF)

    return pl.pallas_call(
        kernel,
        in_specs=[SCALAR, WHOLE],
        out_specs=WHOLE,
        out_shape=shape((ms2, plan.rows_pad)),
        compiler_params=params(),
        cost_estimate=cost(4 * plan.ms * plan.rows * plan.plane, 3e6),
        name="plane_forward",
    )(me, vmem(stack))


def z_forward(plan, me, own, got, table):
    def kernel(_, own_ref, got_ref, table_ref, out_ref, lines, pieces):
        ms = plan.ms
        for g in range(plan.pairs):
            at = slice(g * LANES, (g + 1) * LANES)
            parts = [own_ref[:ms, at], own_ref[ms:, at], got_ref[:ms, at], got_ref[ms:, at]]
            value = dot(jnp.concatenate(parts, 1), table_ref[0])
            for b in (0, 1):
                if 2 * g + b < plan.blocks:
                    lines[2 * g + b] = value[:, b * LANES : (b + 1) * LANES]
        pad = plan.chunk - plan.used
        for i in range(plan.xp):
            for b in range(plan.blocks):
                pieces[i, b * plan.s : (b + 1) * plan.s, :] = lines[b, i * plan.s : (i + 1) * plan.s, :]
            pieces[i, plan.used :, :] = jnp.zeros((pad, LANES), F32)
            out_ref[i] = pieces[i].astype(BF)

    side = (2 * plan.ms, plan.rows_pad)
    return pl.pallas_call(
        kernel,
        grid_spec=pltpu.PrefetchScalarGridSpec(
            num_scalar_prefetch=1,
            grid=(1,),
            in_specs=[
                full(side),
                full(side),
                pl.BlockSpec((1, 4 * LANES, 2 * LANES), lambda t, j: (j[0], 0, 0)),
            ],
            out_specs=full((plan.xp, plan.chunk, LANES)),
            scratch_shapes=[
                pltpu.VMEM((plan.blocks, plan.ms, LANES), F32),
                pltpu.VMEM((plan.xp, plan.chunk, LANES), F32),
            ],
        ),
        out_shape=shape((plan.xp, plan.chunk, LANES)),
        compiler_params=params(),
        cost_estimate=cost(3e8, 1e6),
        name="z_forward",
    )(me, own, got, table)


def x_forward(plan, me, chunks, table):
    def kernel(me_ref, in_ref, table_ref, send_ref, keep_ref, lhs, lines):
        w = plan.width
        for i in range(0, plan.xp, 2):
            first, second = in_ref[i], in_ref[i + 1]
            at = slice(i * w, (i + 2) * w)
            lhs[: plan.chunk, at] = jnp.concatenate([first[:, :w], second[:, :w]], 1)
            lhs[plan.chunk :, at] = jnp.concatenate([first[:, w:], second[:, w:]], 1)
        me = me_ref[0]
        for slot, half, out_ref in ((0, 1 - me, send_ref), (1, me, keep_ref)):
            for r in (0, 1):
                lines[slot, r] = dot(lhs[...], table_ref[half, r])
                for c in range(plan.half):
                    start = (c % 2) * plan.chunk + (c // 2) * plan.s
                    out_ref[c, r] = lines[slot, r, start : start + plan.s, :].astype(BF)

    out = (plan.half, 2, plan.s, plan.modes)
    return pl.pallas_call(
        kernel,
        grid_spec=pltpu.PrefetchScalarGridSpec(
            num_scalar_prefetch=1,
            grid=(1,),
            in_specs=[full((plan.xp, plan.chunk, LANES)), full(table.shape)],
            out_specs=[full(out), full(out)],
            scratch_shapes=[
                pltpu.VMEM((2 * plan.chunk, plan.xp * plan.width), BF),
                pltpu.VMEM((2, 2, 2 * plan.chunk, plan.modes), F32),
            ],
        ),
        out_shape=[shape(out), shape(out)],
        compiler_params=params(),
        cost_estimate=cost(3e8, 3e6),
        name="x_forward",
    )(me, chunks, table)


def mode_product(plan, me, mine, weight, own, got, adjoint):
    def kernel(me_ref, weight_ref, own_ref, got_ref, out_ref, held):
        me = me_ref[0]
        held[me] = own_ref[...].astype(F32)
        held[1 - me] = got_ref[...].astype(F32)
        first = (me if mine else 1 - me) * plan.half

        def one(k, carry):
            real = jnp.zeros((plan.s, plan.modes), F32)
            imag = jnp.zeros((plan.s, plan.modes), F32)
            for c in range(plan.chans):
                pos = (first + k, c) if adjoint else (c, first + k)
                wr = weight_ref[0, pos[0], pos[1]].astype(F32)
                wi = weight_ref[1, pos[0], pos[1]].astype(F32)
                mr = held[c // plan.half, c % plan.half, 0]
                mi = held[c // plan.half, c % plan.half, 1]
                if adjoint:
                    real += wr * mr + wi * mi
                    imag += wr * mi - wi * mr
                else:
                    real += wr * mr - wi * mi
                    imag += wr * mi + wi * mr
            out_ref[k, 0] = real.astype(BF)
            out_ref[k, 1] = imag.astype(BF)
            return carry

        lax.fori_loop(0, plan.half, one, 0)

    side = (plan.half, 2, plan.s, plan.modes)
    return pl.pallas_call(
        kernel,
        in_specs=[SCALAR, WHOLE, WHOLE, WHOLE],
        out_specs=WHOLE,
        out_shape=shape(side),
        scratch_shapes=[pltpu.VMEM((2,) + side, F32)],
        compiler_params=params(),
        cost_estimate=cost(2e9, 4e6),
        name="mode_product",
    )(me, vmem(weight), own, got)


def x_inverse(plan, me, own, got, table, mix):
    carry = mix is not None

    def kernel(me_ref, own_ref, got_ref, table_ref, *rest):
        mix_ref = rest[0] if carry else None
        out_ref, lhs, spare = rest[1:] if carry else rest
        me = me_ref[0]
        pad = plan.chunk - plan.used
        for slot, in_ref in ((0, own_ref), (1, got_ref)):
            for r in (0, 1):
                for c in range(plan.half):
                    start = (c % 2) * plan.chunk + (c // 2) * plan.s
                    lhs[slot, r, start : start + plan.s, :] = in_ref[c, r].astype(F32)
                for c in (0, 1):
                    start = c * plan.chunk + plan.used
                    lhs[slot, r, start : start + pad, :] = jnp.zeros((pad, plan.modes), F32)
        value = None
        for slot, half in ((0, me), (1, 1 - me)):
            for r in (0, 1):
                term = dot(lhs[slot, r].astype(BF), table_ref[half, r])
                value = term if value is None else value + term
        w = plan.width
        if carry:
            spare[...] = jnp.zeros((plan.chunk, LANES), F32)
            spare[plan.used : plan.used + MIX_ROWS, :] = mix_ref[...]
        for i in range(plan.xp):
            first = value[: plan.chunk, i * w : (i + 1) * w]
            second = value[plan.chunk :, i * w : (i + 1) * w]
            piece = jnp.concatenate([first, second], 1)
            if carry:
                piece = piece + spare[...]
            out_ref[i] = piece.astype(BF)

    side = (plan.half, 2, plan.s, plan.modes)
    extra = [full((MIX_ROWS, LANES))] if carry else []
    return pl.pallas_call(
        kernel,
        grid_spec=pltpu.PrefetchScalarGridSpec(
            num_scalar_prefetch=1,
            grid=(1,),
            in_specs=[full(side), full(side), full(table.shape)] + extra,
            out_specs=full((plan.xp, plan.chunk, LANES)),
            scratch_shapes=[
                pltpu.VMEM((2, 2, 2 * plan.chunk, plan.modes), F32),
                pltpu.VMEM((plan.chunk, LANES), F32),
            ],
        ),
        out_shape=shape((plan.xp, plan.chunk, LANES)),
        compiler_params=params(),
        cost_estimate=cost(3e8, 3e6),
        name="x_inverse",
    )(me, own, got, table, *([mix] if carry else []))


def z_inverse(plan, me, chunks, table, carry):
    def kernel(_, in_ref, table_ref, send_ref, keep_ref, *rest):
        mix_ref = rest[0] if carry else None
        lines, pieces = rest[-2:]
        s, ms = plan.s, plan.ms
        for i in range(plan.xp):
            pieces[i] = in_ref[i].astype(F32)
            for b in range(plan.blocks):
                lines[b, i * s : (i + 1) * s, :] = pieces[i, b * s : (b + 1) * s, :]
        for g in range(plan.pairs):
            first = lines[2 * g].astype(BF)
            if 2 * g + 1 < plan.blocks:
                second = lines[2 * g + 1].astype(BF)
            else:
                second = jnp.zeros((ms, LANES), BF)
            value = dot_t(table_ref[0], jnp.concatenate([first, second], 1))
            rows = min(LANES, plan.rows - g * LANES)
            for slot, out_ref in ((0, send_ref), (1, keep_ref)):
                start = 2 * slot * LANES
                both = [value[start : start + rows], value[start + LANES : start + LANES + rows]]
                both = jnp.concatenate(both, 1) * plan.scale
                out_ref[g * LANES : g * LANES + rows, :] = both.astype(BF)
        if carry:
            total = pieces[0, plan.used : plan.used + MIX_ROWS, :]
            for i in range(1, plan.xp):
                total = total + pieces[i, plan.used : plan.used + MIX_ROWS, :]
            per_row = plan.chans // MIX_ROWS
            lane = LANES // per_row
            for c in range(plan.chans):
                row, start = c // per_row, (c % per_row) * lane
                mix_ref[c : c + 1, :] = total[row : row + 1, start : start + plan.chans]

    out = (plan.rows, 2 * plan.ms)
    outs = [out, out]
    out_shape = [shape(out), shape(out)]
    if carry:
        outs.append((plan.chans, plan.chans))
        out_shape.append(shape((plan.chans, plan.chans), F32))
    return pl.pallas_call(
        kernel,
        grid_spec=pltpu.PrefetchScalarGridSpec(
            num_scalar_prefetch=1,
            grid=(1,),
            in_specs=[
                full((plan.xp, plan.chunk, LANES)),
                pl.BlockSpec((1, 4 * LANES, 2 * LANES), lambda t, j: (j[0], 0, 0)),
            ],
            out_specs=[full(o) for o in outs],
            scratch_shapes=[
                pltpu.VMEM((plan.blocks, plan.ms, LANES), F32),
                pltpu.VMEM((plan.xp, plan.chunk, LANES), F32),
            ],
        ),
        out_shape=out_shape,
        compiler_params=params(),
        cost_estimate=cost(3e8, 1e6),
        name="z_inverse",
    )(me, chunks, table)


def mix_blocks(plan, mix, owner):
    cells = 2 * plan.rows

    def kernel(mix_ref, back_ref, owner_ref, owner_t_ref, *outs):
        row = lax.broadcasted_iota(jnp.int32, (plan.rows, cells), 0) % plan.xz
        col = lax.broadcasted_iota(jnp.int32, (plan.rows, cells), 1) % plan.xz
        same = row == col
        for out_ref, ref in zip(outs, (mix_ref, back_ref)):
            for h in (0, 1):
                spread = dot(owner_ref[h * plan.rows : (h + 1) * plan.rows, :], ref[...]).astype(BF)
                wide = dot(spread, owner_t_ref[...])
                out_ref[h] = jnp.where(same, wide, 0.0).astype(BF)

    return pl.pallas_call(
        kernel,
        out_shape=[pltpu.VMEM((2, plan.rows, cells), BF)] * 2,
        compiler_params=params(),
        cost_estimate=cost(4e7, 2e6),
        name="mix_blocks",
    )(mix.T, mix, owner, owner.T)


def gelu_slope(pre):
    size = jnp.abs(pre)
    bell = jnp.exp2(pre * pre * (-0.5 / math.log(2.0)))
    t = 1.0 / (1.0 + size * (0.3275911 / math.sqrt(2.0)))
    poly = 0.5 * 1.061405429
    for coef in (-1.453152027, 1.421413741, -0.284496736, 0.254829592):
        poly = poly * t + 0.5 * coef
    low = bell * (poly * t - size * (1.0 / math.sqrt(2.0 * math.pi)))
    return jnp.where(pre < 0.0, low, 1.0 - low)


def fill_lhs(plan, me, lhs, own_ref, got_ref, mix_ref):
    ms2 = 2 * plan.ms
    for half, in_ref in ((me, own_ref), (1 - me, got_ref)):
        lhs[half, :, :ms2] = in_ref[...]
    for half in (0, 1):
        lhs[half, :, ms2:] = mix_ref[half]


def cells_forward(plan, me, own, got, plane, mixing, stack, cotangent):
    tiles = 2
    width = plan.plane // tiles
    stripe = 32
    ms2 = 2 * plan.ms
    deep = ms2 + 2 * plan.rows
    items = [(t, h) for t in range(tiles) for h in (0, 1)]

    def kernel(
        me_ref, own_ref, got_ref, plane_ref, mix_ref, stack_ref, cot_ref,
        grad_ref, send_ref, keep_ref, lhs, pre, acc, cot, sems,
    ):
        me = me_ref[0]
        copies = []
        for n, (t, h) in enumerate(items):
            at = slice(t * width, (t + 1) * width)
            copies.append(pltpu.make_async_copy(cot_ref.at[h, :, at], cot.at[h, :, at], sems.at[n]))
            copies[-1].start()
        table = pltpu.make_async_copy(plane_ref, grad_ref.at[:ms2, :], sems.at[len(items)])
        table.start()
        fill_lhs(plan, me, lhs, own_ref, got_ref, mix_ref)

        def product(n):
            t, h = items[n]
            pre[n % 2] = dot(lhs[h], stack_ref[:, t * width : (t + 1) * width])

        def slope(n):
            t, h = items[n]
            at = slice(t * width, (t + 1) * width)
            copies[n].wait()
            for r in range(0, plan.rows, stripe):
                value = cot[h, r : r + stripe, at].astype(F32) * gelu_slope(pre[n % 2, r : r + stripe, :])
                start = ms2 + h * plan.rows + r
                grad_ref[start : start + stripe, at] = value.astype(BF)

        def transform(n):
            t, h = items[n]
            at = slice(t * width, (t + 1) * width)
            start = ms2 + h * plan.rows
            value = dot_t(stack_ref[:ms2, at], grad_ref[start : start + plan.rows, at])
            if t == 0:
                acc[h] = value
            else:
                acc[h] += value

        product(0)
        for n in range(len(items)):
            if n + 1 < len(items):
                product(n + 1)
            slope(n)
            if n > 0:
                transform(n - 1)
        transform(len(items) - 1)
        for half, out_ref in ((me, keep_ref), (1 - me, send_ref)):
            pad_lanes(plan, out_ref)
            out_ref[:, : plan.rows] = acc[half].astype(BF)
        table.wait()

    out = (ms2, plan.rows_pad)
    return pl.pallas_call(
        kernel,
        in_specs=[SCALAR, WHOLE, WHOLE, ANYWHERE, WHOLE, WHOLE, ANYWHERE],
        out_specs=[WHOLE] * 3,
        out_shape=[pltpu.VMEM((deep, plan.plane), BF), shape(out), shape(out)],
        scratch_shapes=[
            pltpu.VMEM((2, plan.rows, deep), BF),
            pltpu.VMEM((2, plan.rows, width), F32),
            pltpu.VMEM((2, ms2, plan.rows), F32),
            pltpu.VMEM((2, plan.rows, plan.plane), BF),
            pltpu.SemaphoreType.DMA((len(items) + 1,)),
        ],
        compiler_params=params(),
        cost_estimate=cost(6e9, 1e7),
        name="cells_forward",
    )(me, own, got, hbm(plane), vmem(mixing), vmem(stack), hbm(cotangent.reshape(2, plan.rows, plan.plane)))


def cells_back(plan, me, own, got, mixing, grads):
    tiles = 2
    width = plan.plane // tiles
    ms2 = 2 * plan.ms
    deep = ms2 + 2 * plan.rows
    items = [(t, h) for t in range(tiles) for h in (0, 1)]

    def kernel(me_ref, own_ref, got_ref, mix_ref, grad_ref, out_ref, lhs, held, sems):
        fill_lhs(plan, me_ref[0], lhs, own_ref, got_ref, mix_ref)
        copies = []
        for n, (t, h) in enumerate(items):
            at = slice(t * width, (t + 1) * width)
            held[h, :, at] = dot(lhs[h], grad_ref[:, at]).astype(BF)
            copies.append(pltpu.make_async_copy(held.at[h, :, at], out_ref.at[h, :, at], sems.at[n]))
            copies[-1].start()
        for copy in copies:
            copy.wait()

    cells = (2, plan.rows, plan.plane)
    return pl.pallas_call(
        kernel,
        in_specs=[SCALAR, WHOLE, WHOLE, WHOLE, WHOLE],
        out_specs=ANYWHERE,
        out_shape=shape(cells),
        scratch_shapes=[
            pltpu.VMEM((2, plan.rows, deep), BF),
            pltpu.VMEM(cells, BF),
            pltpu.SemaphoreType.DMA((len(items),)),
        ],
        compiler_params=params(),
        cost_estimate=cost(4e9, 8e6),
        name="cells_back",
    )(me, own, got, vmem(mixing), vmem(grads))


def pack_tables(plan):
    per_row = plan.chans // MIX_ROWS
    lane = LANES // per_row
    assert per_row * MIX_ROWS == plan.chans and lane >= plan.chans
    pick = np.zeros((per_row, MIX_ROWS, plan.chans), np.float32)
    place = np.zeros((per_row, 2 * plan.rows, LANES), np.float32)
    for k in range(per_row):
        for r in range(MIX_ROWS):
            pick[k, r, r * per_row + k] = 1.0
        for cell in range(2 * plan.rows):
            place[k, cell, k * lane + cell // plan.xz] = 1.0
    return pick, place.astype(ml_dtypes.bfloat16)


def mix_partial(plan, stack, grads):
    cells = 2 * plan.rows
    ms2 = 2 * plan.ms
    pick, place = pack_tables(plan)
    factor = 1.0 / math.sqrt(plan.count)

    def kernel(field_ref, grad_ref, pick_ref, place_ref, out_ref, acc):
        acc[...] = dot_t(field_ref[ms2:, :], grad_ref[ms2:, :])
        row = lax.broadcasted_iota(jnp.int32, (plan.xz, cells), 0)
        col = lax.broadcasted_iota(jnp.int32, (plan.xz, cells), 1) % plan.xz
        same = row == col
        lines = []
        for c in range(plan.chans):
            part = jnp.where(same, acc[c * plan.xz : (c + 1) * plan.xz, :], 0.0)
            lines.append(jnp.sum(part, 0, keepdims=True))
        sums = jnp.concatenate(lines, 0) * factor
        high = sums.astype(BF)
        low = (sums - high.astype(F32)).astype(BF)
        total = jnp.zeros((MIX_ROWS, LANES), F32)
        for k in range(plan.chans // MIX_ROWS):
            spread = dot(high, place_ref[k]) + dot(low, place_ref[k])
            total += lax.dot_general(
                pick_ref[k], spread, (((1,), (0,)), ((), ())),
                precision=lax.Precision.HIGHEST, preferred_element_type=F32,
            )
        out_ref[...] = total

    return pl.pallas_call(
        kernel,
        in_specs=[WHOLE] * 4,
        out_specs=WHOLE,
        scratch_shapes=[pltpu.VMEM((cells, cells), F32)],
        out_shape=shape((MIX_ROWS, LANES), F32),
        compiler_params=params(),
        cost_estimate=cost(4e9, 6e6),
        name="mix_partial",
    )(vmem(stack), vmem(grads), pick, place)


def weight_grad(plan, me, field_own, field_got, grad_own, grad_got):
    chans, half = plan.chans, plan.half
    block = 2

    def kernel(me_ref, fo_ref, fg_ref, go_ref, gg_ref, out_ref, plain, turned, real, imag):
        me = me_ref[0]
        step = pl.program_id(0)

        @pl.when(step == 0)
        def _():
            for core, ref in ((me, go_ref), (1 - me, gg_ref)):
                for o in range(half):
                    r, i = ref[o, 0].astype(F32), ref[o, 1].astype(F32)
                    plain[core, o, :, 0, :] = r
                    plain[core, o, :, 1, :] = i
                    turned[core, o, :, 0, :] = i
                    turned[core, o, :, 1, :] = r
            for core, ref in ((me, fo_ref), (1 - me, fg_ref)):
                for c in range(half):
                    r, i = ref[c, 0].astype(F32) * plan.scale, ref[c, 1].astype(F32) * plan.scale
                    real[core, c, :, 0, :] = r
                    real[core, c, :, 1, :] = r
                    imag[core, c, :, 0, :] = i
                    imag[core, c, :, 1, :] = -i

        for k in range(block):
            c = step * block + k
            core = (c >= half).astype(jnp.int32)
            vr, vi = real[core, c - core * half], imag[core, c - core * half]
            for o in range(chans):
                out_ref[k, o] = vr * plain[o // half, o % half] + vi * turned[o // half, o % half]

    side = (half, 2, plan.s, plan.modes)
    held = pltpu.VMEM((2, half, plan.s, 2, plan.modes), F32)
    return pl.pallas_call(
        kernel,
        grid_spec=pltpu.PrefetchScalarGridSpec(
            num_scalar_prefetch=1,
            grid=(chans // block,),
            in_specs=[full(side)] * 4,
            out_specs=pl.BlockSpec((block, chans, plan.s, 2, plan.modes), lambda t, j: (t, 0, 0, 0, 0)),
            scratch_shapes=[held] * 4,
        ),
        out_shape=shape((chans, chans, plan.s, 2, plan.modes), F32),
        compiler_params=params(),
        cost_estimate=cost(8e9, 1.3e7),
        name="weight_grad",
    )(me, field_own, field_got, grad_own, grad_got)


def local(x_parts, z_parts, field, cotangent, spec_weight, mix_weight):
    plan = Plan(field.shape, spec_weight.shape, x_parts, z_parts)
    const = {name: jnp.asarray(value) for name, value in plan.tables().items()}
    core = lax.axis_index("gz").astype(jnp.int32)
    me = core.reshape(1)
    plane = const["plane"]

    def swap(value):
        return lax.ppermute(value, "gz", [(0, 1), (1, 0)])

    def spread(chunks):
        return lax.all_to_all(chunks, "gx", split_axis=0, concat_axis=0, tiled=True)

    def to_modes(keep, got, beside):
        chunks = spread(z_forward(plan, me, keep, got, const["z_forward"]))
        chunks, beside = lax.optimization_barrier((chunks, beside))
        send, own = x_forward(plan, me, chunks, const["x_forward"])
        return own, swap(send), beside

    def product(weight, own, got, adjoint):
        send = mode_product(plan, me, False, weight, own, got, adjoint)
        keep = mode_product(plan, me, True, weight, own, got, adjoint)
        return keep, swap(send)

    def to_cells(keep, got, mix, beside):
        chunks = spread(x_inverse(plan, me, keep, got, const["x_inverse"], mix))
        chunks, beside = lax.optimization_barrier((chunks, beside))
        outs = z_inverse(plan, me, chunks, const["z_inverse"], mix is not None)
        return outs[1], swap(outs[0]), outs[2:], beside

    stack, send = load_forward(plan, me, field, plane)
    got = swap(send)
    keep = plane_forward(plan, me, stack)
    mixing = mix_blocks(plan, mix_weight, const["owner"])
    weight = with_layout_constraint(spec_weight, Layout(major_to_minor=(0, 1, 2, 3, 4)))
    field_own, field_got, (mixing, weight) = to_modes(keep, got, (mixing, weight))
    keep, got = product(weight, field_own, field_got, False)
    keep, got, _, _ = to_cells(keep, got, None, ())
    grads, send, keep = cells_forward(plan, me, keep, got, plane, mixing[0], stack, cotangent)
    partial_mix = mix_partial(plan, stack, grads)
    grad_own, grad_got, partial_mix = to_modes(keep, swap(send), partial_mix)
    partial_mix = partial_mix + swap(partial_mix)
    keep, got = product(weight, grad_own, grad_got, True)
    spec_grad = weight_grad(plan, me, field_own, field_got, grad_own, grad_got)
    keep, got, mix, spec_grad = to_cells(keep, got, partial_mix, spec_grad)
    field_grad = cells_back(plan, me, keep, got, mixing[1], grads).reshape(field.shape)
    return (field_grad, spec_grad.transpose(3, 0, 1, 2, 4), mix[0])


def solution(mesh):
    placed = (
        P(None, ("grp", "gx"), "gz", None),
        P(None, ("grp", "gx"), "gz", None),
        P(None, None, None, "gx", "gz"),
        P(),
    )
    return jax.shard_map(
        functools.partial(local, mesh.shape["gx"], mesh.shape["gz"]),
        mesh=mesh,
        in_specs=placed,
        out_specs=(
            P(None, ("grp", "gx"), "gz", None),
            P("grp", None, None, "gx", "gz"),
            P("grp", None),
        ),
        check_vma=False,
    )
```

```python
import functools
import math

import jax
import jax.numpy as jnp
import ml_dtypes
import numpy as np
from jax import lax
from jax.experimental import pallas as pl
from jax.experimental.layout import Layout, with_layout_constraint
from jax.experimental.pallas import tpu as pltpu
from jax.sharding import PartitionSpec as P

MX = 24
MY = 24
MZ = 16
MT = 8
NY = 128
NSTEP = 16
LANES = 128
MIX_ROWS = 4
BF = jnp.bfloat16
F32 = jnp.float32
VMEM_LIMIT = 18 * 1024 * 1024


def mode_angles(length, count, one_sided):
    cells = np.arange(length)
    ranks = np.arange(count)
    freqs = ranks if one_sided else np.where(ranks < count // 2, ranks, ranks - count)
    wrapped = np.mod(cells[:, None] * freqs[None, :], length)
    return wrapped.astype(np.float32) * np.float32(2.0 * math.pi / length)


def rounded(values):
    return np.asarray(values).astype(np.float32).astype(ml_dtypes.bfloat16).astype(np.float32)


def pair_table(angles, conjugate):
    cosine = rounded(np.cos(angles.astype(np.float64)))
    sine = rounded(np.sin(angles.astype(np.float64)))
    if conjugate:
        rows = [np.stack([cosine, sine], -1), np.stack([-sine, cosine], -1)]
    else:
        rows = [np.stack([cosine, -sine], -1), np.stack([sine, cosine], -1)]
    return np.stack(rows, 1)


def plane_rows():
    y_angle = mode_angles(NY, MY, False)
    t_angle = mode_angles(NSTEP, MT, True)
    total = (y_angle.T[:, None, :, None] + t_angle.T[None, :, None, :]).astype(np.float32)
    total = total.reshape(MY * MT, NY * NSTEP).astype(np.float64)
    return np.concatenate([np.cos(total), -np.sin(total)], 0)


class Plan:
    def __init__(self, field_shape, weight_shape, x_parts, z_parts):
        self.chans, self.xl, self.zl, self.plane = field_shape
        self.xp, self.zp = x_parts, z_parts
        self.x_len, self.z_len = self.xl * x_parts, self.zl * z_parts
        self.half = self.chans // 2
        self.s = weight_shape[3]
        self.modes = weight_shape[4]
        self.kxl = self.modes // MZ
        self.ms = self.s * x_parts
        self.xz = self.xl * self.zl
        self.rows = self.half * self.xz
        self.rows_pad = -(-self.rows // LANES) * LANES
        self.group = LANES // self.xz
        self.pairs = self.rows_pad // LANES
        self.width = self.xl * 2 * MZ
        self.blocks = self.half // 2
        self.used = self.blocks * self.s
        self.chunk = -(-(self.used + MIX_ROWS) // 16) * 16
        self.count = self.x_len * self.z_len * self.plane
        self.scale = 1.0 / self.count
        assert z_parts == 2 and 2 * self.width == LANES and self.group * self.xz == LANES
        assert self.zl == MZ

    def tables(self):
        bf = lambda t: np.ascontiguousarray(t).astype(ml_dtypes.bfloat16)
        g = self.group * self.xl
        eye = np.eye(g, dtype=np.float32)
        zf = pair_table(mode_angles(self.z_len, MZ, False), False)
        zf = zf.reshape(2, self.zl, 2, MZ, 2)
        zf = np.einsum("hzplq,ab->hpazbql", zf, eye).reshape(2, 2 * LANES, 2 * LANES)
        z_forward = np.stack([np.concatenate([zf[0], zf[1]], 0), np.concatenate([zf[1], zf[0]], 0)])
        zi = pair_table(mode_angles(self.z_len, MZ, False), True)
        zi = zi.reshape(2, self.zl, 2, MZ, 2)
        zi = np.einsum("hzplq,ab->hqazbpl", zi, eye).reshape(2, 2 * LANES, 2 * LANES)
        z_inverse = np.stack([np.concatenate([zi[1], zi[0]], 0), np.concatenate([zi[0], zi[1]], 0)])
        eye = np.eye(MZ, dtype=np.float32)
        xf = pair_table(mode_angles(self.x_len, MX, False), False)
        xf = xf.reshape(self.x_len, 2, 2, self.kxl, 2)
        x_forward = np.einsum("xpjkr,ab->jrxpakb", xf, eye)
        x_forward = x_forward.reshape(2, 2, self.xp * self.width, self.modes)
        xi = pair_table(mode_angles(self.x_len, MX, False), True)
        xi = xi.reshape(self.x_len, 2, 2, self.kxl, 2)
        x_inverse = np.einsum("xrjkq,ab->jrkaxqb", xi, eye)
        x_inverse = x_inverse.reshape(2, 2, self.modes, self.xp * self.width)
        owner = np.repeat(np.eye(self.chans, dtype=np.float32), self.xz, axis=0)
        return dict(
            plane=bf(plane_rows()),
            z_forward=bf(z_forward),
            z_inverse=bf(z_inverse),
            x_forward=bf(x_forward),
            x_inverse=bf(x_inverse),
            owner=bf(owner),
        )


def params(**kw):
    return pltpu.CompilerParams(vmem_limit_bytes=VMEM_LIMIT, **kw)


def cost(flops, nbytes):
    return pl.CostEstimate(flops=int(flops), bytes_accessed=int(nbytes), transcendentals=0)


def hbm(value):
    return pltpu.with_memory_space_constraint(value, pltpu.HBM)


def vmem(value):
    return pltpu.with_memory_space_constraint(value, pltpu.VMEM)


WHOLE = pl.BlockSpec(memory_space=pltpu.VMEM)
SCALAR = pl.BlockSpec(memory_space=pltpu.SMEM)
ANYWHERE = pl.BlockSpec(memory_space=pl.ANY)


def shape(dims, kind=BF):
    return jax.ShapeDtypeStruct(tuple(dims), kind)


def full(dims):
    return pl.BlockSpec(tuple(dims), lambda *_: (0,) * len(dims))


def dot(a, b):
    return lax.dot_general(a, b, (((1,), (0,)), ((), ())), preferred_element_type=F32)


def dot_t(a, b):
    return lax.dot_general(a, b, (((1,), (1,)), ((), ())), preferred_element_type=F32)


def pad_lanes(plan, out_ref):
    if plan.rows_pad > plan.rows:
        pad = plan.rows_pad - plan.rows
        out_ref[:, plan.rows :] = jnp.zeros((2 * plan.ms, pad), BF)


def half_rows(plan, half):
    return pl.ds(pl.multiple_of(2 * plan.ms + half * plan.rows, math.gcd(2 * plan.ms, plan.rows)), plan.rows)


def mix_matrix(plan, mix, back, out_ref):
    cells = 2 * plan.rows
    iota = lambda dims, axis: lax.broadcasted_iota(jnp.int32, dims, axis)
    one_hot = lambda hit: hit.astype(F32).astype(BF)
    owner = one_hot(iota((cells, plan.chans), 0) // plan.xz == iota((cells, plan.chans), 1))
    owned = one_hot(iota((plan.chans, cells), 1) // plan.xz == iota((plan.chans, cells), 0))
    spread = (dot if back else dot_t)(owner, mix).astype(BF)
    same = iota((plan.rows, cells), 0) % plan.xz == iota((plan.rows, cells), 1) % plan.xz
    for h in (0, 1):
        wide = dot(spread[h * plan.rows : (h + 1) * plan.rows], owned)
        out_ref[h] = jnp.where(same, wide, 0.0).astype(BF)


def load_forward(plan, me, field, plane, mix):
    tiles = 4
    width = plan.plane // tiles
    ms2 = 2 * plan.ms
    cells = 2 * plan.rows

    def kernel(
        me_ref, field_ref, plane_ref, mix_ref, stack_ref, out_ref, mixing_ref, acc, small, sems, mix_sem,
    ):
        me = me_ref[0]
        copies = []
        for k in range(tiles):
            at = slice(k * width, (k + 1) * width)
            copies.append(
                (
                    pltpu.make_async_copy(plane_ref.at[:, at], stack_ref.at[:ms2, at], sems.at[0, k]),
                    pltpu.make_async_copy(
                        field_ref.at[1 - me, :, at], stack_ref.at[half_rows(plan, 1 - me), at], sems.at[1, k]
                    ),
                    pltpu.make_async_copy(
                        field_ref.at[me, :, at], stack_ref.at[half_rows(plan, me), at], sems.at[2, k]
                    ),
                )
            )
        mix_load = pltpu.make_async_copy(mix_ref, small, mix_sem)
        mix_load.start()
        for group in copies:
            group[0].start()
            group[1].start()
        for group in copies:
            group[2].start()
        mix_load.wait()
        mix_matrix(plan, small[...], False, mixing_ref)
        for k, group in enumerate(copies):
            at = slice(k * width, (k + 1) * width)
            group[0].wait()
            group[1].wait()
            value = dot_t(stack_ref[:ms2, at], stack_ref[half_rows(plan, 1 - me), at])
            if k == 0:
                acc[...] = value
            else:
                acc[...] += value
        pad_lanes(plan, out_ref)
        out_ref[:, : plan.rows] = acc[...].astype(BF)
        for group in copies:
            group[2].wait()

    matrix = pltpu.VMEM((2, plan.rows, cells), BF)
    return pl.pallas_call(
        kernel,
        in_specs=[SCALAR, ANYWHERE, ANYWHERE, ANYWHERE],
        out_specs=[WHOLE, WHOLE, WHOLE],
        out_shape=[pltpu.VMEM((ms2 + cells, plan.plane), BF), shape((ms2, plan.rows_pad)), matrix],
        scratch_shapes=[
            pltpu.VMEM((ms2, plan.rows), F32),
            pltpu.VMEM((plan.chans, plan.chans), BF),
            pltpu.SemaphoreType.DMA((3, tiles)),
            pltpu.SemaphoreType.DMA,
        ],
        compiler_params=params(),
        cost_estimate=cost(4 * plan.ms * plan.rows * plan.plane, 5e6),
        name="load_forward",
    )(me, hbm(field.reshape(2, plan.rows, plan.plane)), hbm(plane), hbm(mix))


def plane_forward(plan, me, stack):
    ms2 = 2 * plan.ms

    def kernel(me_ref, stack_ref, out_ref):
        value = dot_t(stack_ref[:ms2, :], stack_ref[half_rows(plan, me_ref[0]), :])
        pad_lanes(plan, out_ref)
        out_ref[:, : plan.rows] = value.astype(BF)

    return pl.pallas_call(
        kernel,
        in_specs=[SCALAR, WHOLE],
        out_specs=WHOLE,
        out_shape=shape((ms2, plan.rows_pad)),
        compiler_params=params(),
        cost_estimate=cost(4 * plan.ms * plan.rows * plan.plane, 3e6),
        name="plane_forward",
    )(me, vmem(stack))


def z_forward(plan, me, own, got, table):
    def kernel(_, own_ref, got_ref, table_ref, out_ref, lines, pieces):
        ms = plan.ms
        for g in range(plan.pairs):
            at = slice(g * LANES, (g + 1) * LANES)
            parts = [own_ref[:ms, at], own_ref[ms:, at], got_ref[:ms, at], got_ref[ms:, at]]
            value = dot(jnp.concatenate(parts, 1), table_ref[0])
            for b in (0, 1):
                if 2 * g + b < plan.blocks:
                    lines[2 * g + b] = value[:, b * LANES : (b + 1) * LANES]
        pad = plan.chunk - plan.used
        for i in range(plan.xp):
            for b in range(plan.blocks):
                pieces[i, b * plan.s : (b + 1) * plan.s, :] = lines[b, i * plan.s : (i + 1) * plan.s, :]
            pieces[i, plan.used :, :] = jnp.zeros((pad, LANES), F32)
            out_ref[i] = pieces[i].astype(BF)

    side = (2 * plan.ms, plan.rows_pad)
    return pl.pallas_call(
        kernel,
        grid_spec=pltpu.PrefetchScalarGridSpec(
            num_scalar_prefetch=1,
            grid=(1,),
            in_specs=[
                full(side),
                full(side),
                pl.BlockSpec((1, 4 * LANES, 2 * LANES), lambda t, j: (j[0], 0, 0)),
            ],
            out_specs=full((plan.xp, plan.chunk, LANES)),
            scratch_shapes=[
                pltpu.VMEM((plan.blocks, plan.ms, LANES), F32),
                pltpu.VMEM((plan.xp, plan.chunk, LANES), F32),
            ],
        ),
        out_shape=shape((plan.xp, plan.chunk, LANES)),
        compiler_params=params(),
        cost_estimate=cost(3e8, 1e6),
        name="z_forward",
    )(me, own, got, table)


def x_forward(plan, me, chunks, table):
    def kernel(me_ref, in_ref, table_ref, send_ref, keep_ref, lhs, lines):
        w = plan.width
        for i in range(0, plan.xp, 2):
            first, second = in_ref[i], in_ref[i + 1]
            at = slice(i * w, (i + 2) * w)
            lhs[: plan.chunk, at] = jnp.concatenate([first[:, :w], second[:, :w]], 1)
            lhs[plan.chunk :, at] = jnp.concatenate([first[:, w:], second[:, w:]], 1)
        me = me_ref[0]
        for slot, half, out_ref in ((0, 1 - me, send_ref), (1, me, keep_ref)):
            for r in (0, 1):
                lines[slot, r] = dot(lhs[...], table_ref[half, r])
                for c in range(plan.half):
                    start = (c % 2) * plan.chunk + (c // 2) * plan.s
                    out_ref[c, r] = lines[slot, r, start : start + plan.s, :].astype(BF)

    out = (plan.half, 2, plan.s, plan.modes)
    return pl.pallas_call(
        kernel,
        grid_spec=pltpu.PrefetchScalarGridSpec(
            num_scalar_prefetch=1,
            grid=(1,),
            in_specs=[full((plan.xp, plan.chunk, LANES)), full(table.shape)],
            out_specs=[full(out), full(out)],
            scratch_shapes=[
                pltpu.VMEM((2 * plan.chunk, plan.xp * plan.width), BF),
                pltpu.VMEM((2, 2, 2 * plan.chunk, plan.modes), F32),
            ],
        ),
        out_shape=[shape(out), shape(out)],
        compiler_params=params(),
        cost_estimate=cost(3e8, 3e6),
        name="x_forward",
    )(me, chunks, table)


def mode_sums(plan, weight_ref, held, out_ref, adjoint, arrive, start=0):
    def one(k, carry):
        arrive(k)
        real = jnp.zeros((plan.s, plan.modes), F32)
        imag = jnp.zeros((plan.s, plan.modes), F32)
        for c in range(plan.chans):
            pos = (start + k, c) if adjoint else (c, start + k)
            wr = weight_ref[0, pos[0], pos[1]].astype(F32)
            wi = weight_ref[1, pos[0], pos[1]].astype(F32)
            mr = held[c // plan.half, c % plan.half, 0]
            mi = held[c // plan.half, c % plan.half, 1]
            if adjoint:
                real += wr * mr + wi * mi
                imag += wr * mi - wi * mr
            else:
                real += wr * mr - wi * mi
                imag += wr * mi + wi * mr
        out_ref[k, 0] = real.astype(BF)
        out_ref[k, 1] = imag.astype(BF)
        return carry

    lax.fori_loop(0, plan.half, one, 0)


def mode_product(plan, me, weight, own, got, adjoint):
    side = (plan.half, 2, plan.s, plan.modes)
    if adjoint:
        part = (2, plan.half, plan.chans, plan.s, plan.modes)
    else:
        part = (2, plan.chans, plan.half, plan.s, plan.modes)
    held = pltpu.VMEM((2,) + side, F32)

    def hold(me, held, own_ref, got_ref):
        held[me] = own_ref[...].astype(F32)
        held[1 - me] = got_ref[...].astype(F32)

    def first(me_ref, weight_ref, own_ref, got_ref, out_ref, rest_ref, held, part_ref, sems):
        me = me_ref[0]

        def copy(k, half, to, sem):
            if adjoint:
                return pltpu.make_async_copy(weight_ref.at[:, half * plan.half + k], to.at[:, k], sem)
            return pltpu.make_async_copy(weight_ref.at[:, :, half * plan.half + k], to.at[:, :, k], sem)

        for k in range(plan.half):
            copy(k, 1 - me, part_ref, sems.at[0, k]).start()
        for k in range(plan.half):
            copy(k, me, rest_ref, sems.at[1, k]).start()
        hold(me, held, own_ref, got_ref)
        arrive = lambda k: copy(k, 1 - me, part_ref, sems.at[0, k]).wait()
        mode_sums(plan, part_ref, held, out_ref, adjoint, arrive)
        for k in range(plan.half):
            copy(k, me, rest_ref, sems.at[1, k]).wait()

    def second(me_ref, weight_ref, own_ref, got_ref, out_ref, held):
        hold(me_ref[0], held, own_ref, got_ref)
        mode_sums(plan, weight_ref, held, out_ref, adjoint, lambda k: None)

    def resident(mine, me_ref, weight_ref, own_ref, got_ref, out_ref, held):
        me = me_ref[0]
        hold(me, held, own_ref, got_ref)
        start = (me if mine else 1 - me) * plan.half
        mode_sums(plan, weight_ref, held, out_ref, adjoint, lambda k: None, start)

    if not adjoint:
        return [
            pl.pallas_call(
                functools.partial(resident, mine),
                in_specs=[SCALAR, WHOLE, WHOLE, WHOLE],
                out_specs=WHOLE,
                out_shape=shape(side),
                scratch_shapes=[held],
                compiler_params=params(),
                cost_estimate=cost(2e9, 4e6),
                name="mode_product",
            )(me, vmem(weight), own, got)
            for mine in (False, True)
        ]

    send, rest = pl.pallas_call(
        first,
        in_specs=[SCALAR, ANYWHERE, WHOLE, WHOLE],
        out_specs=[WHOLE, WHOLE],
        out_shape=[shape(side), pltpu.VMEM(part, BF)],
        scratch_shapes=[held, pltpu.VMEM(part, BF), pltpu.SemaphoreType.DMA((2, plan.half))],
        compiler_params=params(),
        cost_estimate=cost(2e9, 6e6),
        name="mode_product_send",
    )(me, hbm(weight), own, got)
    keep = pl.pallas_call(
        second,
        in_specs=[SCALAR, WHOLE, WHOLE, WHOLE],
        out_specs=WHOLE,
        out_shape=shape(side),
        scratch_shapes=[held],
        compiler_params=params(),
        cost_estimate=cost(2e9, 4e6),
        name="mode_product_keep",
    )(me, vmem(rest), own, got)
    return send, keep


def x_inverse(plan, me, own, got, table, mix):
    carry = mix is not None

    def kernel(me_ref, own_ref, got_ref, table_ref, *rest):
        mix_ref = rest[0] if carry else None
        out_ref, lhs, spare = rest[1:] if carry else rest
        me = me_ref[0]
        pad = plan.chunk - plan.used
        for slot, in_ref in ((0, own_ref), (1, got_ref)):
            for r in (0, 1):
                for c in range(plan.half):
                    start = (c % 2) * plan.chunk + (c // 2) * plan.s
                    lhs[slot, r, start : start + plan.s, :] = in_ref[c, r].astype(F32)
                for c in (0, 1):
                    start = c * plan.chunk + plan.used
                    lhs[slot, r, start : start + pad, :] = jnp.zeros((pad, plan.modes), F32)
        value = None
        for slot, half in ((0, me), (1, 1 - me)):
            for r in (0, 1):
                term = dot(lhs[slot, r].astype(BF), table_ref[half, r])
                value = term if value is None else value + term
        w = plan.width
        if carry:
            spare[...] = jnp.zeros((plan.chunk, LANES), F32)
            spare[plan.used : plan.used + MIX_ROWS, :] = mix_ref[...]
        for i in range(plan.xp):
            first = value[: plan.chunk, i * w : (i + 1) * w]
            second = value[plan.chunk :, i * w : (i + 1) * w]
            piece = jnp.concatenate([first, second], 1)
            if carry:
                piece = piece + spare[...]
            out_ref[i] = piece.astype(BF)

    side = (plan.half, 2, plan.s, plan.modes)
    extra = [full((MIX_ROWS, LANES))] if carry else []
    return pl.pallas_call(
        kernel,
        grid_spec=pltpu.PrefetchScalarGridSpec(
            num_scalar_prefetch=1,
            grid=(1,),
            in_specs=[full(side), full(side), full(table.shape)] + extra,
            out_specs=full((plan.xp, plan.chunk, LANES)),
            scratch_shapes=[
                pltpu.VMEM((2, 2, 2 * plan.chunk, plan.modes), F32),
                pltpu.VMEM((plan.chunk, LANES), F32),
            ],
        ),
        out_shape=shape((plan.xp, plan.chunk, LANES)),
        compiler_params=params(),
        cost_estimate=cost(3e8, 3e6),
        name="x_inverse",
    )(me, own, got, table, *([mix] if carry else []))


def z_inverse(plan, me, chunks, table, carry):
    def kernel(_, in_ref, table_ref, send_ref, keep_ref, *rest):
        mix_ref = rest[0] if carry else None
        lines, pieces = rest[-2:]
        s, ms = plan.s, plan.ms
        for i in range(plan.xp):
            pieces[i] = in_ref[i].astype(F32)
            for b in range(plan.blocks):
                lines[b, i * s : (i + 1) * s, :] = pieces[i, b * s : (b + 1) * s, :]
        for g in range(plan.pairs):
            first = lines[2 * g].astype(BF)
            if 2 * g + 1 < plan.blocks:
                second = lines[2 * g + 1].astype(BF)
            else:
                second = jnp.zeros((ms, LANES), BF)
            value = dot_t(table_ref[0], jnp.concatenate([first, second], 1))
            rows = min(LANES, plan.rows - g * LANES)
            for slot, out_ref in ((0, send_ref), (1, keep_ref)):
                start = 2 * slot * LANES
                both = [value[start : start + rows], value[start + LANES : start + LANES + rows]]
                both = jnp.concatenate(both, 1) * plan.scale
                out_ref[g * LANES : g * LANES + rows, :] = both.astype(BF)
        if carry:
            total = pieces[0, plan.used : plan.used + MIX_ROWS, :]
            for i in range(1, plan.xp):
                total = total + pieces[i, plan.used : plan.used + MIX_ROWS, :]
            mix_ref[...] = total
            high = total.astype(BF).astype(F32)
            fill = jnp.zeros((16 - 2 * MIX_ROWS, LANES), F32)
            send_ref[plan.rows :, :] = jnp.zeros((16, 2 * ms), BF)
            send_ref[plan.rows :, :LANES] = jnp.concatenate([high, total - high, fill], 0).astype(BF)

    out = (plan.rows, 2 * plan.ms)
    sent = (plan.rows + 16, 2 * plan.ms) if carry else out
    outs = [sent, out]
    out_shape = [shape(sent), shape(out)]
    if carry:
        outs.append((MIX_ROWS, LANES))
        out_shape.append(shape((MIX_ROWS, LANES), F32))
    return pl.pallas_call(
        kernel,
        grid_spec=pltpu.PrefetchScalarGridSpec(
            num_scalar_prefetch=1,
            grid=(1,),
            in_specs=[
                full((plan.xp, plan.chunk, LANES)),
                pl.BlockSpec((1, 4 * LANES, 2 * LANES), lambda t, j: (j[0], 0, 0)),
            ],
            out_specs=[full(o) for o in outs],
            scratch_shapes=[
                pltpu.VMEM((plan.blocks, plan.ms, LANES), F32),
                pltpu.VMEM((plan.xp, plan.chunk, LANES), F32),
            ],
        ),
        out_shape=out_shape,
        compiler_params=params(),
        cost_estimate=cost(3e8, 1e6),
        name="z_inverse",
    )(me, chunks, table)


def tile_loads(plan, tiles, source, target, sems):
    width = plan.plane // tiles
    groups = []
    for k in range(tiles):
        at = slice(k * width, (k + 1) * width)
        rows = [slice(h * plan.rows, (h + 1) * plan.rows) for h in (0, 1)]
        groups.append(
            [pltpu.make_async_copy(source.at[h, :, at], target.at[rows[h], at], sems.at[h, k]) for h in (0, 1)]
        )
    return groups


def gelu_slope(pre):
    size = jnp.abs(pre)
    bell = jnp.exp2(pre * pre * (-0.5 / math.log(2.0)))
    t = 1.0 / (1.0 + size * (0.3275911 / math.sqrt(2.0)))
    poly = 0.5 * 1.061405429
    for coef in (-1.453152027, 1.421413741, -0.284496736, 0.254829592):
        poly = poly * t + 0.5 * coef
    low = bell * (poly * t - size * (1.0 / math.sqrt(2.0 * math.pi)))
    return jnp.where(pre < 0.0, low, 1.0 - low)


def cells_forward(plan, me, modes, mixing, stack, cotangent, before):
    tiles = 4
    width = plan.plane // tiles
    stripe = 32
    ms2 = 2 * plan.ms
    first = before is None

    def kernel(me_ref, modes_ref, mix_ref, stack_ref, cot_ref, *rest):
        if first:
            grad, out_ref, pre, acc = rest
            half = me_ref[0]
        else:
            before_ref, grad_ref, out_ref, pre, acc, grad, sems = rest
            half = 1 - me_ref[0]
            stores = [pltpu.make_async_copy(before_ref, grad_ref.at[1 - half], sems.at[tiles])]
            stores[0].start()
        lhs = jnp.concatenate([modes_ref[...], mix_ref[half]], 1)

        def product(k):
            pre[k % 2] = dot(lhs, stack_ref[:, k * width : (k + 1) * width])

        def slope(k):
            at = slice(k * width, (k + 1) * width)
            for r in range(0, plan.rows, stripe):
                rows = slice(r, r + stripe)
                value = cot_ref[half, rows, at].astype(F32) * gelu_slope(pre[k % 2, rows, :])
                grad[rows, at] = value.astype(BF)
            if not first:
                stores.append(pltpu.make_async_copy(grad.at[:, at], grad_ref.at[half, :, at], sems.at[k]))
                stores[-1].start()

        def transform(k):
            at = slice(k * width, (k + 1) * width)
            value = dot_t(stack_ref[:ms2, at], grad[:, at])
            if k == 0:
                acc[...] = value
            else:
                acc[...] += value

        product(0)
        for k in range(tiles):
            if k + 1 < tiles:
                product(k + 1)
            slope(k)
            if k > 0:
                transform(k - 1)
        transform(tiles - 1)
        pad_lanes(plan, out_ref)
        out_ref[:, : plan.rows] = acc[...].astype(BF)
        if not first:
            for store in stores:
                store.wait()

    out = (ms2, plan.rows_pad)
    cells = (2, plan.rows, plan.plane)
    half = pltpu.VMEM((plan.rows, plan.plane), BF)
    return pl.pallas_call(
        kernel,
        in_specs=[SCALAR] + [WHOLE] * (4 if first else 5),
        out_specs=[WHOLE if first else ANYWHERE, WHOLE],
        out_shape=[half if first else pltpu.HBM(cells, BF), shape(out)],
        scratch_shapes=[pltpu.VMEM((2, plan.rows, width), F32), pltpu.VMEM((ms2, plan.rows), F32)]
        + ([] if first else [half, pltpu.SemaphoreType.DMA((tiles + 1,))]),
        compiler_params=params(),
        cost_estimate=cost(3e9, 5e6),
        name="cells_forward_own" if first else "cells_forward_got",
    )(
        me, modes, vmem(mixing), vmem(stack), vmem(cotangent.reshape(cells)),
        *([] if first else [vmem(before)]),
    )


def cells_back(plan, me, modes, plane, mixing, grads, before, mix_sums):
    tiles = 4
    width = plan.plane // tiles
    per_row = plan.chans // MIX_ROWS
    lane = LANES // per_row
    first = before is None

    def kernel(me_ref, modes_ref, plane_in, mix_ref, grad_in, *rest):
        if first:
            held, grad_ref, plane_ref, sems, plane_sems = rest
            half = me_ref[0]
            loads = tile_loads(plan, tiles, grad_in, grad_ref, sems)
            for k, group in enumerate(loads):
                at = slice(k * width, (k + 1) * width)
                group.append(pltpu.make_async_copy(plane_in.at[:, at], plane_ref.at[:, at], plane_sems.at[k]))
                for copy in group:
                    copy.start()
        else:
            before_ref, sums_ref, out_ref, mix_out, held, sums, sems = rest
            grad_ref, plane_ref = grad_in, plane_in
            half = 1 - me_ref[0]
            stores = [pltpu.make_async_copy(before_ref, out_ref.at[1 - half], sems.at[tiles])]
            stores[0].start()
        lhs = jnp.concatenate([modes_ref[: plan.rows], mix_ref[half]], 1)
        for k in range(tiles):
            at = slice(k * width, (k + 1) * width)
            if first:
                for copy in loads[k]:
                    copy.wait()
            value = dot(lhs, jnp.concatenate([plane_ref[:, at], grad_ref[:, at]], 0))
            held[:, at] = value.astype(BF)
            if not first:
                stores.append(pltpu.make_async_copy(held.at[:, at], out_ref.at[half, :, at], sems.at[k]))
                stores[-1].start()
        if not first:
            sums[...] = modes_ref[plan.rows :, :LANES].astype(F32)
            total = sums_ref[...] + sums[:MIX_ROWS, :] + sums[MIX_ROWS : 2 * MIX_ROWS, :]
            for c in range(plan.chans):
                row, start = c // per_row, (c % per_row) * lane
                mix_out[c : c + 1, :] = total[row : row + 1, start : start + plan.chans]
            for store in stores:
                store.wait()

    half = pltpu.VMEM((plan.rows, plan.plane), BF)
    whole = pltpu.VMEM((2 * plan.rows, plan.plane), BF)
    if first:
        outs, out_specs = [half, whole, pltpu.VMEM(plane.shape, BF)], [WHOLE] * 3
        scratch = [pltpu.SemaphoreType.DMA((2, tiles)), pltpu.SemaphoreType.DMA((tiles,))]
    else:
        outs = [pltpu.HBM((2, plan.rows, plan.plane), BF), shape((plan.chans, plan.chans), F32)]
        out_specs = [ANYWHERE, WHOLE]
        scratch = [half, pltpu.VMEM((16, LANES), F32), pltpu.SemaphoreType.DMA((tiles + 1,))]
    return pl.pallas_call(
        kernel,
        in_specs=[SCALAR, WHOLE, ANYWHERE, WHOLE, ANYWHERE] if first else [SCALAR] + [WHOLE] * 6,
        out_specs=out_specs,
        out_shape=outs,
        scratch_shapes=scratch,
        compiler_params=params(),
        cost_estimate=cost(2e9, 4e6),
        name="cells_back_own" if first else "cells_back_got",
    )(
        me, modes, hbm(plane) if first else vmem(plane), vmem(mixing), hbm(grads) if first else vmem(grads),
        *([] if first else [vmem(before), mix_sums]),
    )


def mix_partial(plan, mix, owner, field, grads):
    tiles = 4
    width = plan.plane // tiles
    cells = 2 * plan.rows
    per_row = plan.chans // MIX_ROWS
    lane = LANES // per_row
    assert per_row * MIX_ROWS == plan.chans and lane > plan.chans
    factor = 1.0 / math.sqrt(plan.count)

    def kernel(mix_ref, owner_ref, field_in, grad_in, out_ref, mixing_ref, acc, field_ref, grad_ref, sums, matrix, sems, mix_sem):
        loads = zip(tile_loads(plan, tiles, grad_in, grad_ref, sems.at[0]), tile_loads(plan, tiles, field_in, field_ref, sems.at[1]))
        loads = [first + second for first, second in loads]
        for group in loads:
            for copy in group:
                copy.start()
        mix_matrix(plan, mix_ref[...], True, matrix)
        mix_store = pltpu.make_async_copy(matrix, mixing_ref, mix_sem)
        mix_store.start()
        for k in range(tiles):
            at = slice(k * width, (k + 1) * width)
            for copy in loads[k]:
                copy.wait()
            value = dot_t(field_ref[:, at], grad_ref[:, at])
            if k == 0:
                acc[...] = value
            else:
                acc[...] += value
        row = lax.broadcasted_iota(jnp.int32, (plan.xz, cells), 0)
        col = lax.broadcasted_iota(jnp.int32, (plan.xz, cells), 1) % plan.xz
        same = row == col
        lines = []
        for c in range(plan.chans):
            part = jnp.where(same, acc[c * plan.xz : (c + 1) * plan.xz, :], 0.0)
            lines.append(jnp.sum(part, 0, keepdims=True))
        line = jnp.concatenate(lines, 0) * factor
        high = line.astype(BF)
        low = (line - high.astype(F32)).astype(BF)
        sums[...] = dot(high, owner_ref[...]) + dot(low, owner_ref[...])
        out_ref[...] = jnp.zeros((MIX_ROWS, LANES), F32)
        for c in range(plan.chans):
            at, start = c // per_row, (c % per_row) * lane
            out_ref[at : at + 1, start : start + plan.chans] = sums[c : c + 1, :]
        mix_store.wait()

    return pl.pallas_call(
        kernel,
        in_specs=[WHOLE, WHOLE, ANYWHERE, ANYWHERE],
        out_specs=[WHOLE, ANYWHERE],
        out_shape=[shape((MIX_ROWS, LANES), F32), pltpu.HBM((2, plan.rows, cells), BF)],
        scratch_shapes=[
            pltpu.VMEM((cells, cells), F32),
            pltpu.VMEM((cells, plan.plane), BF),
            pltpu.VMEM((cells, plan.plane), BF),
            pltpu.VMEM((plan.chans, plan.chans), F32),
            pltpu.VMEM((2, plan.rows, cells), BF),
            pltpu.SemaphoreType.DMA((2, 2, tiles)),
            pltpu.SemaphoreType.DMA,
        ],
        compiler_params=params(),
        cost_estimate=cost(4e9, 6e6),
        name="mix_partial",
    )(mix, owner, hbm(field.reshape(2, plan.rows, plan.plane)), hbm(grads))


def weight_grad(plan, me, field_own, field_got, grad_own, grad_got):
    chans, half = plan.chans, plan.half
    block = 2

    def kernel(me_ref, fo_ref, fg_ref, go_ref, gg_ref, out_ref, plain, turned, real, imag):
        me = me_ref[0]
        step = pl.program_id(0)

        @pl.when(step == 0)
        def _():
            for core, ref in ((me, go_ref), (1 - me, gg_ref)):
                for o in range(half):
                    r, i = ref[o, 0].astype(F32), ref[o, 1].astype(F32)
                    plain[core, o, :, 0, :] = r
                    plain[core, o, :, 1, :] = i
                    turned[core, o, :, 0, :] = i
                    turned[core, o, :, 1, :] = r
            for core, ref in ((me, fo_ref), (1 - me, fg_ref)):
                for c in range(half):
                    r, i = ref[c, 0].astype(F32) * plan.scale, ref[c, 1].astype(F32) * plan.scale
                    real[core, c, :, 0, :] = r
                    real[core, c, :, 1, :] = r
                    imag[core, c, :, 0, :] = i
                    imag[core, c, :, 1, :] = -i

        for k in range(block):
            c = step * block + k
            core = (c >= half).astype(jnp.int32)
            vr, vi = real[core, c - core * half], imag[core, c - core * half]
            for o in range(chans):
                out_ref[k, o] = vr * plain[o // half, o % half] + vi * turned[o // half, o % half]

    side = (half, 2, plan.s, plan.modes)
    held = pltpu.VMEM((2, half, plan.s, 2, plan.modes), F32)
    return pl.pallas_call(
        kernel,
        grid_spec=pltpu.PrefetchScalarGridSpec(
            num_scalar_prefetch=1,
            grid=(chans // block,),
            in_specs=[full(side)] * 4,
            out_specs=pl.BlockSpec((block, chans, plan.s, 2, plan.modes), lambda t, j: (t, 0, 0, 0, 0)),
            scratch_shapes=[held] * 4,
        ),
        out_shape=shape((chans, chans, plan.s, 2, plan.modes), F32),
        compiler_params=params(),
        cost_estimate=cost(8e9, 1.3e7),
        name="weight_grad",
    )(me, field_own, field_got, grad_own, grad_got)


def local(x_parts, z_parts, field, cotangent, spec_weight, mix_weight):
    plan = Plan(field.shape, spec_weight.shape, x_parts, z_parts)
    const = {name: jnp.asarray(value) for name, value in plan.tables().items()}
    core = lax.axis_index("gz").astype(jnp.int32)
    me = core.reshape(1)
    plane = const["plane"]

    def swap(value):
        return lax.ppermute(value, "gz", [(0, 1), (1, 0)])

    def spread(chunks):
        return lax.all_to_all(chunks, "gx", split_axis=0, concat_axis=0, tiled=True)

    def to_modes(keep, got, beside):
        chunks = spread(z_forward(plan, me, keep, got, const["z_forward"]))
        chunks, beside = lax.optimization_barrier((chunks, beside))
        send, own = x_forward(plan, me, chunks, const["x_forward"])
        return own, swap(send), beside

    def product(weight, own, got, adjoint):
        send, keep = mode_product(plan, me, weight, own, got, adjoint)
        return keep, swap(send)

    def to_cells(keep, got, mix, beside):
        chunks = spread(x_inverse(plan, me, keep, got, const["x_inverse"], mix))
        chunks, beside = lax.optimization_barrier((chunks, beside))
        outs = z_inverse(plan, me, chunks, const["z_inverse"], mix is not None)
        return outs[1], swap(outs[0]), outs[2:], beside

    stack, send, mixing = load_forward(plan, me, field, plane, mix_weight)
    got = swap(send)
    keep = plane_forward(plan, me, stack)
    weight = with_layout_constraint(spec_weight, Layout(major_to_minor=(0, 1, 2, 3, 4)))
    field_own, field_got, _ = to_modes(keep, got, ())
    keep, got = product(weight, field_own, field_got, False)
    keep, got, _, _ = to_cells(keep, got, None, ())
    before, keep = cells_forward(plan, me, keep, mixing, stack, cotangent, None)
    grads, send = cells_forward(plan, me, got, mixing, stack, cotangent, before)
    beside = mix_partial(plan, mix_weight, const["owner"], field, grads)
    grad_own, grad_got, (partial_mix, mixing) = to_modes(keep, swap(send), beside)
    keep, got = product(weight, grad_own, grad_got, True)
    spec_grad = weight_grad(plan, me, field_own, field_got, grad_own, grad_got)
    keep, got, mix, spec_grad = to_cells(keep, got, partial_mix, spec_grad)
    before, grads, table = cells_back(plan, me, keep, plane, mixing, grads, None, None)
    field_grad, mix_grad = cells_back(plan, me, got, table, mixing, grads, before, mix[0])
    return (field_grad.reshape(field.shape), spec_grad.transpose(3, 0, 1, 2, 4), mix_grad)


def solution(mesh):
    placed = (
        P(None, ("grp", "gx"), "gz", None),
        P(None, ("grp", "gx"), "gz", None),
        P(None, None, None, "gx", "gz"),
        P(),
    )
    return jax.shard_map(
        functools.partial(local, mesh.shape["gx"], mesh.shape["gz"]),
        mesh=mesh,
        in_specs=placed,
        out_specs=(
            P(None, ("grp", "gx"), "gz", None),
            P("grp", None, None, "gx", "gz"),
            P("grp", None),
        ),
        check_vma=False,
    )
```

```python
import functools
import math

import jax
import jax.numpy as jnp
import ml_dtypes
import numpy as np
from jax import lax
from jax.experimental import pallas as pl
from jax.experimental.layout import Layout, with_layout_constraint
from jax.experimental.pallas import tpu as pltpu
from jax.sharding import PartitionSpec as P

MX = 24
MY = 24
MZ = 16
MT = 8
NY = 128
NSTEP = 16
LANES = 128
MIX_ROWS = 4
BF = jnp.bfloat16
F32 = jnp.float32
VMEM_LIMIT = 18 * 1024 * 1024


def mode_angles(length, count, one_sided):
    cells = np.arange(length)
    ranks = np.arange(count)
    freqs = ranks if one_sided else np.where(ranks < count // 2, ranks, ranks - count)
    wrapped = np.mod(cells[:, None] * freqs[None, :], length)
    return wrapped.astype(np.float32) * np.float32(2.0 * math.pi / length)


def rounded(values):
    return np.asarray(values).astype(np.float32).astype(ml_dtypes.bfloat16).astype(np.float32)


def pair_table(angles, conjugate):
    cosine = rounded(np.cos(angles.astype(np.float64)))
    sine = rounded(np.sin(angles.astype(np.float64)))
    if conjugate:
        rows = [np.stack([cosine, sine], -1), np.stack([-sine, cosine], -1)]
    else:
        rows = [np.stack([cosine, -sine], -1), np.stack([sine, cosine], -1)]
    return np.stack(rows, 1)


def plane_rows():
    y_angle = mode_angles(NY, MY, False)
    t_angle = mode_angles(NSTEP, MT, True)
    total = (y_angle.T[:, None, :, None] + t_angle.T[None, :, None, :]).astype(np.float32)
    total = total.reshape(MY * MT, NY * NSTEP).astype(np.float64)
    return np.concatenate([np.cos(total), -np.sin(total)], 0)


class Plan:
    def __init__(self, field_shape, weight_shape, x_parts, z_parts):
        self.chans, self.xl, self.zl, self.plane = field_shape
        self.xp, self.zp = x_parts, z_parts
        self.x_len, self.z_len = self.xl * x_parts, self.zl * z_parts
        self.half = self.chans // 2
        self.s = weight_shape[3]
        self.modes = weight_shape[4]
        self.kxl = self.modes // MZ
        self.ms = self.s * x_parts
        self.xz = self.xl * self.zl
        self.rows = self.half * self.xz
        self.rows_pad = -(-self.rows // LANES) * LANES
        self.group = LANES // self.xz
        self.pairs = self.rows_pad // LANES
        self.width = self.xl * 2 * MZ
        self.blocks = self.half // 2
        self.used = self.blocks * self.s
        self.chunk = -(-(self.used + MIX_ROWS) // 16) * 16
        self.count = self.x_len * self.z_len * self.plane
        self.scale = 1.0 / self.count
        assert z_parts == 2 and 2 * self.width == LANES and self.group * self.xz == LANES
        assert self.zl == MZ

    def tables(self):
        bf = lambda t: np.ascontiguousarray(t).astype(ml_dtypes.bfloat16)
        g = self.group * self.xl
        eye = np.eye(g, dtype=np.float32)
        zf = pair_table(mode_angles(self.z_len, MZ, False), False)
        zf = zf.reshape(2, self.zl, 2, MZ, 2)
        zf = np.einsum("hzplq,ab->hpazbql", zf, eye).reshape(2, 2 * LANES, 2 * LANES)
        z_forward = np.stack([np.concatenate([zf[0], zf[1]], 0), np.concatenate([zf[1], zf[0]], 0)])
        zi = pair_table(mode_angles(self.z_len, MZ, False), True)
        zi = zi.reshape(2, self.zl, 2, MZ, 2)
        zi = np.einsum("hzplq,ab->hqazbpl", zi, eye).reshape(2, 2 * LANES, 2 * LANES)
        z_inverse = np.stack([np.concatenate([zi[1], zi[0]], 0), np.concatenate([zi[0], zi[1]], 0)])
        eye = np.eye(MZ, dtype=np.float32)
        xf = pair_table(mode_angles(self.x_len, MX, False), False)
        xf = xf.reshape(self.x_len, 2, 2, self.kxl, 2)
        x_forward = np.einsum("xpjkr,ab->jrxpakb", xf, eye)
        x_forward = x_forward.reshape(2, 2, self.xp * self.width, self.modes)
        xi = pair_table(mode_angles(self.x_len, MX, False), True)
        xi = xi.reshape(self.x_len, 2, 2, self.kxl, 2)
        x_inverse = np.einsum("xrjkq,ab->jrkaxqb", xi, eye)
        x_inverse = x_inverse.reshape(2, 2, self.modes, self.xp * self.width)
        owner = np.repeat(np.eye(self.chans, dtype=np.float32), self.xz, axis=0)
        return dict(
            plane=bf(plane_rows()),
            z_forward=bf(z_forward),
            z_inverse=bf(z_inverse),
            x_forward=bf(x_forward),
            x_inverse=bf(x_inverse),
            owner=bf(owner),
        )


def params(**kw):
    return pltpu.CompilerParams(vmem_limit_bytes=VMEM_LIMIT, **kw)


def cost(flops, nbytes):
    return pl.CostEstimate(flops=int(flops), bytes_accessed=int(nbytes), transcendentals=0)


def hbm(value):
    return pltpu.with_memory_space_constraint(value, pltpu.HBM)


def vmem(value):
    return pltpu.with_memory_space_constraint(value, pltpu.VMEM)


WHOLE = pl.BlockSpec(memory_space=pltpu.VMEM)
SCALAR = pl.BlockSpec(memory_space=pltpu.SMEM)
ANYWHERE = pl.BlockSpec(memory_space=pl.ANY)


def shape(dims, kind=BF):
    return jax.ShapeDtypeStruct(tuple(dims), kind)


def full(dims):
    return pl.BlockSpec(tuple(dims), lambda *_: (0,) * len(dims))


def dot(a, b):
    return lax.dot_general(a, b, (((1,), (0,)), ((), ())), preferred_element_type=F32)


def dot_t(a, b):
    return lax.dot_general(a, b, (((1,), (1,)), ((), ())), preferred_element_type=F32)


def pad_lanes(plan, out_ref):
    if plan.rows_pad > plan.rows:
        pad = plan.rows_pad - plan.rows
        out_ref[:, plan.rows :] = jnp.zeros((2 * plan.ms, pad), BF)


def half_rows(plan, half):
    return pl.ds(pl.multiple_of(2 * plan.ms + half * plan.rows, math.gcd(2 * plan.ms, plan.rows)), plan.rows)


def mix_masks(plan, owned_ref, mask_ref, wide_ref):
    cells = 2 * plan.rows
    shift = plan.xz.bit_length() - 1
    assert 1 << shift == plan.xz
    iota = lambda dims, axis: lax.broadcasted_iota(jnp.int32, dims, axis)
    mine = (iota((plan.chans, cells), 1) >> shift) == iota((plan.chans, cells), 0)
    owned_ref[...] = jnp.where(mine, 1.0, 0.0).astype(BF)
    apart = (iota((plan.xz, cells), 0) - iota((plan.xz, cells), 1)) & (plan.xz - 1)
    mask_ref[...] = jnp.where(apart == 0, 1.0, 0.0).astype(F32)


def mix_matrix(plan, mix, back, owned_ref, mask_ref, wide_ref, out_ref):
    sides = (((1,), (0,)), ((), ())) if back else (((0,), (0,)), ((), ()))
    wide_ref[...] = lax.dot_general(mix, owned_ref[...], sides, preferred_element_type=F32)
    for c in range(plan.chans):
        half, start = c // plan.half, (c % plan.half) * plan.xz
        line = wide_ref[c : c + 1, :] * mask_ref[...]
        out_ref[half, start : start + plan.xz, :] = line.astype(BF)


def mix_scratch(plan):
    cells = 2 * plan.rows
    return [pltpu.VMEM((plan.chans, cells), BF), pltpu.VMEM((plan.xz, cells), F32), pltpu.VMEM((plan.chans, cells), F32)]


def load_forward(plan, me, field, plane, mix):
    tiles = 4
    width = plan.plane // tiles
    ms2 = 2 * plan.ms
    cells = 2 * plan.rows

    def kernel(
        me_ref, field_ref, plane_ref, mix_ref, stack_ref, out_ref, mixing_ref,
        acc, small, sems, mix_sem, *masks,
    ):
        me = me_ref[0]
        copies = []
        for k in range(tiles):
            at = slice(k * width, (k + 1) * width)
            copies.append(
                (
                    pltpu.make_async_copy(plane_ref.at[:, at], stack_ref.at[:ms2, at], sems.at[0, k]),
                    pltpu.make_async_copy(
                        field_ref.at[1 - me, :, at], stack_ref.at[half_rows(plan, 1 - me), at], sems.at[1, k]
                    ),
                    pltpu.make_async_copy(
                        field_ref.at[me, :, at], stack_ref.at[half_rows(plan, me), at], sems.at[2, k]
                    ),
                )
            )
        mix_load = pltpu.make_async_copy(mix_ref, small, mix_sem)
        mix_load.start()
        for group in copies:
            group[0].start()
            group[1].start()
        for group in copies:
            group[2].start()
        mix_masks(plan, *masks)
        for k, group in enumerate(copies):
            at = slice(k * width, (k + 1) * width)
            group[0].wait()
            group[1].wait()
            value = dot_t(stack_ref[:ms2, at], stack_ref[half_rows(plan, 1 - me), at])
            if k == 0:
                acc[...] = value
            else:
                acc[...] += value
        pad_lanes(plan, out_ref)
        out_ref[:, : plan.rows] = acc[...].astype(BF)
        mix_load.wait()
        mix_matrix(plan, small[...], False, *masks, mixing_ref)
        for group in copies:
            group[2].wait()

    matrix = pltpu.VMEM((2, plan.rows, cells), BF)
    return pl.pallas_call(
        kernel,
        in_specs=[SCALAR, ANYWHERE, ANYWHERE, ANYWHERE],
        out_specs=[WHOLE, WHOLE, WHOLE],
        out_shape=[pltpu.VMEM((ms2 + cells, plan.plane), BF), shape((ms2, plan.rows_pad)), matrix],
        scratch_shapes=[
            pltpu.VMEM((ms2, plan.rows), F32),
            pltpu.VMEM((plan.chans, plan.chans), BF),
            pltpu.SemaphoreType.DMA((3, tiles)),
            pltpu.SemaphoreType.DMA,
        ]
        + mix_scratch(plan),
        compiler_params=params(),
        cost_estimate=cost(4 * plan.ms * plan.rows * plan.plane, 5e6),
        name="load_forward",
    )(me, hbm(field.reshape(2, plan.rows, plan.plane)), hbm(plane), hbm(mix))


def plane_forward(plan, me, stack, spec_weight):
    ms2 = 2 * plan.ms
    tiles = 4
    native = spec_weight.transpose(1, 2, 3, 0, 4)
    step = plan.chans // tiles

    def kernel(me_ref, stack_ref, weight_in, out_ref, weight_ref, sems):
        loads = []
        for k in range(tiles):
            at = slice(k * step, (k + 1) * step)
            loads.append(pltpu.make_async_copy(weight_in.at[at], weight_ref.at[at], sems.at[k]))
            loads[-1].start()
        value = dot_t(stack_ref[:ms2, :], stack_ref[half_rows(plan, me_ref[0]), :])
        pad_lanes(plan, out_ref)
        out_ref[:, : plan.rows] = value.astype(BF)
        for load in loads:
            load.wait()

    keep, native = pl.pallas_call(
        kernel,
        in_specs=[SCALAR, WHOLE, ANYWHERE],
        out_specs=[WHOLE, WHOLE],
        out_shape=[shape((ms2, plan.rows_pad)), pltpu.VMEM(native.shape, BF)],
        scratch_shapes=[pltpu.SemaphoreType.DMA((tiles,))],
        compiler_params=params(),
        cost_estimate=cost(4 * plan.ms * plan.rows * plan.plane, 3e6),
        name="plane_forward",
    )(me, vmem(stack), hbm(native))
    return keep, native.transpose(3, 0, 1, 2, 4)


def z_forward(plan, me, own, got, table):
    def kernel(_, own_ref, got_ref, table_ref, out_ref, lines, pieces):
        ms = plan.ms
        for g in range(plan.pairs):
            at = slice(g * LANES, (g + 1) * LANES)
            parts = [own_ref[:ms, at], own_ref[ms:, at], got_ref[:ms, at], got_ref[ms:, at]]
            value = dot(jnp.concatenate(parts, 1), table_ref[0])
            for b in (0, 1):
                if 2 * g + b < plan.blocks:
                    lines[2 * g + b] = value[:, b * LANES : (b + 1) * LANES]
        pad = plan.chunk - plan.used
        for i in range(plan.xp):
            for b in range(plan.blocks):
                pieces[i, b * plan.s : (b + 1) * plan.s, :] = lines[b, i * plan.s : (i + 1) * plan.s, :]
            pieces[i, plan.used :, :] = jnp.zeros((pad, LANES), F32)
            out_ref[i] = pieces[i].astype(BF)

    side = (2 * plan.ms, plan.rows_pad)
    return pl.pallas_call(
        kernel,
        grid_spec=pltpu.PrefetchScalarGridSpec(
            num_scalar_prefetch=1,
            grid=(1,),
            in_specs=[
                full(side),
                full(side),
                pl.BlockSpec((1, 4 * LANES, 2 * LANES), lambda t, j: (j[0], 0, 0)),
            ],
            out_specs=full((plan.xp, plan.chunk, LANES)),
            scratch_shapes=[
                pltpu.VMEM((plan.blocks, plan.ms, LANES), F32),
                pltpu.VMEM((plan.xp, plan.chunk, LANES), F32),
            ],
        ),
        out_shape=shape((plan.xp, plan.chunk, LANES)),
        compiler_params=params(),
        cost_estimate=cost(3e8, 1e6),
        name="z_forward",
    )(me, own, got, table)


def x_forward(plan, me, chunks, table):
    def kernel(me_ref, in_ref, table_ref, send_ref, keep_ref, lhs, lines):
        w = plan.width
        for i in range(0, plan.xp, 2):
            first, second = in_ref[i], in_ref[i + 1]
            at = slice(i * w, (i + 2) * w)
            lhs[: plan.chunk, at] = jnp.concatenate([first[:, :w], second[:, :w]], 1)
            lhs[plan.chunk :, at] = jnp.concatenate([first[:, w:], second[:, w:]], 1)
        me = me_ref[0]
        for slot, half, out_ref in ((0, 1 - me, send_ref), (1, me, keep_ref)):
            for r in (0, 1):
                lines[slot, r] = dot(lhs[...], table_ref[half, r])
                for c in range(plan.half):
                    start = (c % 2) * plan.chunk + (c // 2) * plan.s
                    out_ref[c, r] = lines[slot, r, start : start + plan.s, :].astype(BF)

    out = (plan.half, 2, plan.s, plan.modes)
    return pl.pallas_call(
        kernel,
        grid_spec=pltpu.PrefetchScalarGridSpec(
            num_scalar_prefetch=1,
            grid=(1,),
            in_specs=[full((plan.xp, plan.chunk, LANES)), full(table.shape)],
            out_specs=[full(out), full(out)],
            scratch_shapes=[
                pltpu.VMEM((2 * plan.chunk, plan.xp * plan.width), BF),
                pltpu.VMEM((2, 2, 2 * plan.chunk, plan.modes), F32),
            ],
        ),
        out_shape=[shape(out), shape(out)],
        compiler_params=params(),
        cost_estimate=cost(3e8, 3e6),
        name="x_forward",
    )(me, chunks, table)


def mode_product(plan, me, mine, weight, own, got, adjoint):
    def kernel(me_ref, weight_ref, own_ref, got_ref, out_ref, held):
        me = me_ref[0]
        held[me] = own_ref[...].astype(F32)
        held[1 - me] = got_ref[...].astype(F32)
        start = (me if mine else 1 - me) * plan.half

        def one(k, carry):
            real = jnp.zeros((plan.s, plan.modes), F32)
            imag = jnp.zeros((plan.s, plan.modes), F32)
            for c in range(plan.chans):
                pos = (start + k, c) if adjoint else (c, start + k)
                wr = weight_ref[0, pos[0], pos[1]].astype(F32)
                wi = weight_ref[1, pos[0], pos[1]].astype(F32)
                mr = held[c // plan.half, c % plan.half, 0]
                mi = held[c // plan.half, c % plan.half, 1]
                if adjoint:
                    real += wr * mr + wi * mi
                    imag += wr * mi - wi * mr
                else:
                    real += wr * mr - wi * mi
                    imag += wr * mi + wi * mr
            out_ref[k, 0] = real.astype(BF)
            out_ref[k, 1] = imag.astype(BF)
            return carry

        lax.fori_loop(0, plan.half, one, 0)

    side = (plan.half, 2, plan.s, plan.modes)
    return pl.pallas_call(
        kernel,
        in_specs=[SCALAR, WHOLE, WHOLE, WHOLE],
        out_specs=WHOLE,
        out_shape=shape(side),
        scratch_shapes=[pltpu.VMEM((2,) + side, F32)],
        compiler_params=params(),
        cost_estimate=cost(2e9, 4e6),
        name="mode_product",
    )(me, vmem(weight), own, got)


def x_inverse(plan, me, own, got, table, mix):
    carry = mix is not None

    def kernel(me_ref, own_ref, got_ref, table_ref, *rest):
        mix_ref = rest[0] if carry else None
        out_ref, lhs, spare = rest[1:] if carry else rest
        me = me_ref[0]
        pad = plan.chunk - plan.used
        for slot, in_ref in ((0, own_ref), (1, got_ref)):
            for r in (0, 1):
                for c in range(plan.half):
                    start = (c % 2) * plan.chunk + (c // 2) * plan.s
                    lhs[slot, r, start : start + plan.s, :] = in_ref[c, r].astype(F32)
                for c in (0, 1):
                    start = c * plan.chunk + plan.used
                    lhs[slot, r, start : start + pad, :] = jnp.zeros((pad, plan.modes), F32)
        value = None
        for slot, half in ((0, me), (1, 1 - me)):
            for r in (0, 1):
                term = dot(lhs[slot, r].astype(BF), table_ref[half, r])
                value = term if value is None else value + term
        w = plan.width
        if carry:
            spare[...] = jnp.zeros((plan.chunk, LANES), F32)
            spare[plan.used : plan.used + MIX_ROWS, :] = mix_ref[...]
        for i in range(plan.xp):
            first = value[: plan.chunk, i * w : (i + 1) * w]
            second = value[plan.chunk :, i * w : (i + 1) * w]
            piece = jnp.concatenate([first, second], 1)
            if carry:
                piece = piece + spare[...]
            out_ref[i] = piece.astype(BF)

    side = (plan.half, 2, plan.s, plan.modes)
    extra = [full((MIX_ROWS, LANES))] if carry else []
    return pl.pallas_call(
        kernel,
        grid_spec=pltpu.PrefetchScalarGridSpec(
            num_scalar_prefetch=1,
            grid=(1,),
            in_specs=[full(side), full(side), full(table.shape)] + extra,
            out_specs=full((plan.xp, plan.chunk, LANES)),
            scratch_shapes=[
                pltpu.VMEM((2, 2, 2 * plan.chunk, plan.modes), F32),
                pltpu.VMEM((plan.chunk, LANES), F32),
            ],
        ),
        out_shape=shape((plan.xp, plan.chunk, LANES)),
        compiler_params=params(),
        cost_estimate=cost(3e8, 3e6),
        name="x_inverse",
    )(me, own, got, table, *([mix] if carry else []))


def z_inverse(plan, me, chunks, table, carry):
    def kernel(_, in_ref, table_ref, send_ref, keep_ref, *rest):
        mix_ref = rest[0] if carry else None
        lines, pieces = rest[-2:]
        s, ms = plan.s, plan.ms
        for i in range(plan.xp):
            pieces[i] = in_ref[i].astype(F32)
            for b in range(plan.blocks):
                lines[b, i * s : (i + 1) * s, :] = pieces[i, b * s : (b + 1) * s, :]
        for g in range(plan.pairs):
            first = lines[2 * g].astype(BF)
            if 2 * g + 1 < plan.blocks:
                second = lines[2 * g + 1].astype(BF)
            else:
                second = jnp.zeros((ms, LANES), BF)
            value = dot_t(table_ref[0], jnp.concatenate([first, second], 1))
            rows = min(LANES, plan.rows - g * LANES)
            for slot, out_ref in ((0, send_ref), (1, keep_ref)):
                start = 2 * slot * LANES
                both = [value[start : start + rows], value[start + LANES : start + LANES + rows]]
                both = jnp.concatenate(both, 1) * plan.scale
                out_ref[g * LANES : g * LANES + rows, :] = both.astype(BF)
        if carry:
            total = pieces[0, plan.used : plan.used + MIX_ROWS, :]
            for i in range(1, plan.xp):
                total = total + pieces[i, plan.used : plan.used + MIX_ROWS, :]
            mix_ref[...] = total
            high = total.astype(BF).astype(F32)
            fill = jnp.zeros((16 - 2 * MIX_ROWS, LANES), F32)
            send_ref[plan.rows :, :] = jnp.zeros((16, 2 * ms), BF)
            send_ref[plan.rows :, :LANES] = jnp.concatenate([high, total - high, fill], 0).astype(BF)

    out = (plan.rows, 2 * plan.ms)
    sent = (plan.rows + 16, 2 * plan.ms) if carry else out
    outs = [sent, out]
    out_shape = [shape(sent), shape(out)]
    if carry:
        outs.append((MIX_ROWS, LANES))
        out_shape.append(shape((MIX_ROWS, LANES), F32))
    return pl.pallas_call(
        kernel,
        grid_spec=pltpu.PrefetchScalarGridSpec(
            num_scalar_prefetch=1,
            grid=(1,),
            in_specs=[
                full((plan.xp, plan.chunk, LANES)),
                pl.BlockSpec((1, 4 * LANES, 2 * LANES), lambda t, j: (j[0], 0, 0)),
            ],
            out_specs=[full(o) for o in outs],
            scratch_shapes=[
                pltpu.VMEM((plan.blocks, plan.ms, LANES), F32),
                pltpu.VMEM((plan.xp, plan.chunk, LANES), F32),
            ],
        ),
        out_shape=out_shape,
        compiler_params=params(),
        cost_estimate=cost(3e8, 1e6),
        name="z_inverse",
    )(me, chunks, table)


def tile_loads(plan, tiles, source, target, sems):
    width = plan.plane // tiles
    groups = []
    for k in range(tiles):
        at = slice(k * width, (k + 1) * width)
        rows = [slice(h * plan.rows, (h + 1) * plan.rows) for h in (0, 1)]
        groups.append(
            [pltpu.make_async_copy(source.at[h, :, at], target.at[rows[h], at], sems.at[h, k]) for h in (0, 1)]
        )
    return groups


def gelu_slope(pre):
    size = jnp.abs(pre)
    bell = jnp.exp2(pre * pre * (-0.5 / math.log(2.0)))
    t = 1.0 / (1.0 + size * (0.3275911 / math.sqrt(2.0)))
    poly = 0.5 * 1.061405429
    for coef in (-1.453152027, 1.421413741, -0.284496736, 0.254829592):
        poly = poly * t + 0.5 * coef
    low = bell * (poly * t - size * (1.0 / math.sqrt(2.0 * math.pi)))
    return jnp.where(pre < 0.0, low, 1.0 - low)


def cells_forward(plan, me, modes, mixing, stack, cotangent, before):
    tiles = 4
    width = plan.plane // tiles
    stripe = 32
    ms2 = 2 * plan.ms
    first = before is None

    def kernel(me_ref, modes_ref, mix_ref, stack_ref, cot_ref, *rest):
        if first:
            grad, out_ref, pre, acc = rest
            half = me_ref[0]
        else:
            before_ref, grad_ref, out_ref, grad, pre, acc, sems = rest
            half = 1 - me_ref[0]
            stores = [pltpu.make_async_copy(before_ref, grad_ref.at[1 - half], sems.at[tiles])]
            stores[0].start()
        lhs = jnp.concatenate([modes_ref[...], mix_ref[half]], 1)

        def product(k):
            pre[k % 2] = dot(lhs, stack_ref[:, k * width : (k + 1) * width])

        def slope(k):
            at = slice(k * width, (k + 1) * width)
            for r in range(0, plan.rows, stripe):
                rows = slice(r, r + stripe)
                value = cot_ref[half, rows, at].astype(F32) * gelu_slope(pre[k % 2, rows, :])
                grad[rows, at] = value.astype(BF)
            if not first:
                stores.append(pltpu.make_async_copy(grad.at[:, at], grad_ref.at[half, :, at], sems.at[k]))
                stores[-1].start()

        def transform(k):
            at = slice(k * width, (k + 1) * width)
            value = dot_t(stack_ref[:ms2, at], grad[:, at])
            if k == 0:
                acc[...] = value
            else:
                acc[...] += value

        product(0)
        for k in range(tiles):
            if k + 1 < tiles:
                product(k + 1)
            slope(k)
            if k > 0:
                transform(k - 1)
        transform(tiles - 1)
        pad_lanes(plan, out_ref)
        out_ref[:, : plan.rows] = acc[...].astype(BF)
        if not first:
            for store in stores:
                store.wait()

    out = (ms2, plan.rows_pad)
    cells = (2, plan.rows, plan.plane)
    half = pltpu.VMEM((plan.rows, plan.plane), BF)
    return pl.pallas_call(
        kernel,
        in_specs=[SCALAR] + [WHOLE] * (4 if first else 5),
        out_specs=[WHOLE, WHOLE] if first else [ANYWHERE, WHOLE, WHOLE],
        out_shape=[half, shape(out)] if first else [pltpu.HBM(cells, BF), shape(out), half],
        scratch_shapes=[pltpu.VMEM((2, plan.rows, width), F32), pltpu.VMEM((ms2, plan.rows), F32)]
        + ([] if first else [pltpu.SemaphoreType.DMA((tiles + 1,))]),
        compiler_params=params(),
        cost_estimate=cost(3e9, 5e6),
        name="cells_forward_own" if first else "cells_forward_got",
    )(
        me, modes, vmem(mixing), vmem(stack), vmem(cotangent.reshape(cells)),
        *([] if first else [vmem(before)]),
    )


def cells_back(plan, me, modes, plane, mixing, grads, before, mix_sums):
    tiles = 4
    width = plan.plane // tiles
    per_row = plan.chans // MIX_ROWS
    lane = LANES // per_row
    first = before is None

    def kernel(me_ref, modes_ref, plane_in, mix_ref, grad_in, *rest):
        if first:
            held, grad_ref, plane_ref, matrix, sems, plane_sems, *masks = rest
            half = me_ref[0]
            loads = tile_loads(plan, tiles, grad_in, grad_ref, sems)
            for k, group in enumerate(loads):
                at = slice(k * width, (k + 1) * width)
                group.append(pltpu.make_async_copy(plane_in.at[:, at], plane_ref.at[:, at], plane_sems.at[k]))
                for copy in group:
                    copy.start()
            mix_masks(plan, *masks)
            mix_matrix(plan, mix_ref[...], True, *masks, matrix)
        else:
            before_ref, sums_ref, out_ref, mix_out, held, sums, sems = rest
            matrix = mix_ref
            grad_ref, plane_ref = grad_in, plane_in
            half = 1 - me_ref[0]
            stores = [pltpu.make_async_copy(before_ref, out_ref.at[1 - half], sems.at[tiles])]
            stores[0].start()
        lhs = jnp.concatenate([modes_ref[: plan.rows], matrix[half]], 1)
        for k in range(tiles):
            at = slice(k * width, (k + 1) * width)
            if first:
                for copy in loads[k]:
                    copy.wait()
            value = dot(lhs, jnp.concatenate([plane_ref[:, at], grad_ref[:, at]], 0))
            held[:, at] = value.astype(BF)
            if not first:
                stores.append(pltpu.make_async_copy(held.at[:, at], out_ref.at[half, :, at], sems.at[k]))
                stores[-1].start()
        if not first:
            sums[...] = modes_ref[plan.rows :, :LANES].astype(F32)
            total = sums_ref[...] + sums[:MIX_ROWS, :] + sums[MIX_ROWS : 2 * MIX_ROWS, :]
            for c in range(plan.chans):
                row, start = c // per_row, (c % per_row) * lane
                mix_out[c : c + 1, :] = total[row : row + 1, start : start + plan.chans]
            for store in stores:
                store.wait()

    half = pltpu.VMEM((plan.rows, plan.plane), BF)
    whole = pltpu.VMEM((2 * plan.rows, plan.plane), BF)
    if first:
        outs = [half, whole, pltpu.VMEM(plane.shape, BF), pltpu.VMEM((2, plan.rows, 2 * plan.rows), BF)]
        out_specs = [WHOLE] * 4
        scratch = [pltpu.SemaphoreType.DMA((2, tiles)), pltpu.SemaphoreType.DMA((tiles,))] + mix_scratch(plan)
    else:
        outs = [pltpu.HBM((2, plan.rows, plan.plane), BF), shape((plan.chans, plan.chans), F32)]
        out_specs = [ANYWHERE, WHOLE]
        scratch = [half, pltpu.VMEM((16, LANES), F32), pltpu.SemaphoreType.DMA((tiles + 1,))]
    return pl.pallas_call(
        kernel,
        in_specs=[SCALAR, WHOLE, ANYWHERE, WHOLE, ANYWHERE] if first else [SCALAR] + [WHOLE] * 6,
        out_specs=out_specs,
        out_shape=outs,
        scratch_shapes=scratch,
        compiler_params=params(),
        cost_estimate=cost(2e9, 4e6),
        name="cells_back_own" if first else "cells_back_got",
    )(
        me, modes, hbm(plane) if first else vmem(plane), mixing if first else vmem(mixing), hbm(grads) if first else vmem(grads),
        *([] if first else [vmem(before), mix_sums]),
    )


def mix_partial(plan, me, owner, stack, grad, before):
    cells = 2 * plan.rows
    ms2 = 2 * plan.ms
    per_row = plan.chans // MIX_ROWS
    lane = LANES // per_row
    assert per_row * MIX_ROWS == plan.chans and lane > plan.chans
    factor = 1.0 / math.sqrt(plan.count)
    first = before is None

    def kernel(me_ref, owner_ref, stack_ref, grad_ref, *rest):
        acc = rest[-1] if first else rest[-2]
        acc[...] = dot_t(stack_ref[ms2:, :], grad_ref[...])
        iota = lambda axis: lax.broadcasted_iota(jnp.int32, (plan.xz, plan.rows), axis)
        apart = (iota(0) - iota(1)) & (plan.xz - 1)
        lines = []
        for c in range(plan.chans):
            part = jnp.where(apart == 0, acc[c * plan.xz : (c + 1) * plan.xz, :], 0.0)
            lines.append(jnp.sum(part, 0, keepdims=True))
        line = jnp.concatenate(lines, 0) * factor
        high = line.astype(BF)
        low = (line - high.astype(F32)).astype(BF)
        owned = owner_ref[: plan.rows, : plan.half]
        value = dot(high, owned) + dot(low, owned)
        if first:
            rest[0][...] = value
            return
        before_ref, out_ref, _, sums = rest
        swapped = me_ref[0] == 0
        sums[:, : plan.half] = jnp.where(swapped, before_ref[...], value)
        sums[:, plan.half :] = jnp.where(swapped, value, before_ref[...])
        out_ref[...] = jnp.zeros((MIX_ROWS, LANES), F32)
        for c in range(plan.chans):
            at, start = c // per_row, (c % per_row) * lane
            out_ref[at : at + 1, start : start + plan.chans] = sums[c : c + 1, :]

    return pl.pallas_call(
        kernel,
        in_specs=[SCALAR] + [WHOLE] * (3 if first else 4),
        out_specs=WHOLE,
        out_shape=shape((plan.chans, plan.half) if first else (MIX_ROWS, LANES), F32),
        scratch_shapes=[pltpu.VMEM((cells, plan.rows), F32)]
        + ([] if first else [pltpu.VMEM((plan.chans, plan.chans), F32)]),
        compiler_params=params(),
        cost_estimate=cost(2e9, 4e6),
        name="mix_partial_own" if first else "mix_partial_got",
    )(me, owner, vmem(stack), vmem(grad), *([] if first else [before]))


def weight_grad(plan, me, field_own, field_got, grad_own, grad_got):
    chans, half = plan.chans, plan.half
    block = 2

    def kernel(me_ref, fo_ref, fg_ref, go_ref, gg_ref, out_ref, plain, turned, real, imag):
        me = me_ref[0]
        step = pl.program_id(0)

        @pl.when(step == 0)
        def _():
            for core, ref in ((me, go_ref), (1 - me, gg_ref)):
                for o in range(half):
                    r, i = ref[o, 0].astype(F32), ref[o, 1].astype(F32)
                    plain[core, o, :, 0, :] = r
                    plain[core, o, :, 1, :] = i
                    turned[core, o, :, 0, :] = i
                    turned[core, o, :, 1, :] = r
            for core, ref in ((me, fo_ref), (1 - me, fg_ref)):
                for c in range(half):
                    r, i = ref[c, 0].astype(F32) * plan.scale, ref[c, 1].astype(F32) * plan.scale
                    real[core, c, :, 0, :] = r
                    real[core, c, :, 1, :] = r
                    imag[core, c, :, 0, :] = i
                    imag[core, c, :, 1, :] = -i

        for k in range(block):
            c = step * block + k
            core = (c >= half).astype(jnp.int32)
            vr, vi = real[core, c - core * half], imag[core, c - core * half]
            for o in range(chans):
                out_ref[k, o] = vr * plain[o // half, o % half] + vi * turned[o // half, o % half]

    side = (half, 2, plan.s, plan.modes)
    held = pltpu.VMEM((2, half, plan.s, 2, plan.modes), F32)
    return pl.pallas_call(
        kernel,
        grid_spec=pltpu.PrefetchScalarGridSpec(
            num_scalar_prefetch=1,
            grid=(chans // block,),
            in_specs=[full(side)] * 4,
            out_specs=pl.BlockSpec((block, chans, plan.s, 2, plan.modes), lambda t, j: (t, 0, 0, 0, 0)),
            scratch_shapes=[held] * 4,
        ),
        out_shape=shape((chans, chans, plan.s, 2, plan.modes), F32),
        compiler_params=params(),
        cost_estimate=cost(8e9, 1.3e7),
        name="weight_grad",
    )(me, field_own, field_got, grad_own, grad_got)


def local(x_parts, z_parts, field, cotangent, spec_weight, mix_weight):
    plan = Plan(field.shape, spec_weight.shape, x_parts, z_parts)
    const = {name: jnp.asarray(value) for name, value in plan.tables().items()}
    core = lax.axis_index("gz").astype(jnp.int32)
    me = core.reshape(1)
    plane = const["plane"]


    def swap(value):
        return lax.ppermute(value, "gz", [(0, 1), (1, 0)])

    def spread(chunks):
        return lax.all_to_all(chunks, "gx", split_axis=0, concat_axis=0, tiled=True)

    def to_modes(keep, got):
        chunks = spread(z_forward(plan, me, keep, got, const["z_forward"]))
        send, own = x_forward(plan, me, chunks, const["x_forward"])
        return own, swap(send)

    def product(own, got, adjoint):
        send = mode_product(plan, me, False, weight, own, got, adjoint)
        keep = mode_product(plan, me, True, weight, own, got, adjoint)
        return keep, swap(send)

    def to_cells(keep, got, mix, beside):
        chunks = spread(x_inverse(plan, me, keep, got, const["x_inverse"], mix))
        chunks, beside = lax.optimization_barrier((chunks, beside))
        outs = z_inverse(plan, me, chunks, const["z_inverse"], mix is not None)
        return outs[1], swap(outs[0]), outs[2:], beside

    stack, send, mixing = load_forward(plan, me, field, plane, mix_weight)
    got = swap(send)
    keep, weight = plane_forward(plan, me, stack, spec_weight)
    field_own, field_got = to_modes(keep, got)
    keep, got = product(field_own, field_got, False)
    keep, got, _, _ = to_cells(keep, got, None, ())
    grad_own, keep = cells_forward(plan, me, keep, mixing, stack, cotangent, None)
    grads, send, grad_got = cells_forward(plan, me, got, mixing, stack, cotangent, grad_own)
    got = swap(send)
    partial_mix = mix_partial(plan, me, const["owner"], stack, grad_own, None)
    got, partial_mix = lax.optimization_barrier((got, partial_mix))
    grad_own, got = to_modes(keep, got)
    partial_mix = mix_partial(plan, me, const["owner"], stack, grad_got, partial_mix)
    got, partial_mix = lax.optimization_barrier((got, partial_mix))
    grad_got = got
    keep, got = product(grad_own, grad_got, True)
    spec_grad = weight_grad(plan, me, field_own, field_got, grad_own, grad_got)
    keep, got, mix, spec_grad = to_cells(keep, got, partial_mix, spec_grad)
    before, grads, table, mixing = cells_back(plan, me, keep, plane, mix_weight, grads, None, None)
    field_grad, mix_grad = cells_back(plan, me, got, table, mixing, grads, before, mix[0])
    return (field_grad.reshape(field.shape), spec_grad.transpose(3, 0, 1, 2, 4), mix_grad)


def solution(mesh):
    placed = (
        P(None, ("grp", "gx"), "gz", None),
        P(None, ("grp", "gx"), "gz", None),
        P(None, None, None, "gx", "gz"),
        P(),
    )
    return jax.shard_map(
        functools.partial(local, mesh.shape["gx"], mesh.shape["gz"]),
        mesh=mesh,
        in_specs=placed,
        out_specs=(
            P(None, ("grp", "gx"), "gz", None),
            P("grp", None, None, "gx", "gz"),
            P("grp", None),
        ),
        check_vma=False,
    )
```

```python
import functools
import math

import jax
import jax.numpy as jnp
import ml_dtypes
import numpy as np
from jax import lax
from jax.experimental import pallas as pl
from jax.experimental.layout import Layout, with_layout_constraint
from jax.experimental.pallas import tpu as pltpu
from jax.sharding import PartitionSpec as P

MX = 24
MY = 24
MZ = 16
MT = 8
NY = 128
NSTEP = 16
LANES = 128
MIX_ROWS = 4
BF = jnp.bfloat16
F32 = jnp.float32
VMEM_LIMIT = 18 * 1024 * 1024


def mode_angles(length, count, one_sided):
    cells = np.arange(length)
    ranks = np.arange(count)
    freqs = ranks if one_sided else np.where(ranks < count // 2, ranks, ranks - count)
    wrapped = np.mod(cells[:, None] * freqs[None, :], length)
    return wrapped.astype(np.float32) * np.float32(2.0 * math.pi / length)


def rounded(values):
    return np.asarray(values).astype(np.float32).astype(ml_dtypes.bfloat16).astype(np.float32)


def pair_table(angles, conjugate):
    cosine = rounded(np.cos(angles.astype(np.float64)))
    sine = rounded(np.sin(angles.astype(np.float64)))
    if conjugate:
        rows = [np.stack([cosine, sine], -1), np.stack([-sine, cosine], -1)]
    else:
        rows = [np.stack([cosine, -sine], -1), np.stack([sine, cosine], -1)]
    return np.stack(rows, 1)


def plane_rows():
    y_angle = mode_angles(NY, MY, False)
    t_angle = mode_angles(NSTEP, MT, True)
    total = (y_angle.T[:, None, :, None] + t_angle.T[None, :, None, :]).astype(np.float32)
    total = total.reshape(MY * MT, NY * NSTEP).astype(np.float64)
    return np.concatenate([np.cos(total), -np.sin(total)], 0)


class Plan:
    def __init__(self, field_shape, weight_shape, x_parts, z_parts):
        self.chans, self.xl, self.zl, self.plane = field_shape
        self.xp, self.zp = x_parts, z_parts
        self.x_len, self.z_len = self.xl * x_parts, self.zl * z_parts
        self.half = self.chans // 2
        self.s = weight_shape[3]
        self.modes = weight_shape[4]
        self.kxl = self.modes // MZ
        self.ms = self.s * x_parts
        self.xz = self.xl * self.zl
        self.rows = self.half * self.xz
        self.rows_pad = -(-self.rows // LANES) * LANES
        self.group = LANES // self.xz
        self.pairs = self.rows_pad // LANES
        self.width = self.xl * 2 * MZ
        self.blocks = self.half // 2
        self.used = self.blocks * self.s
        self.chunk = -(-(self.used + MIX_ROWS) // 16) * 16
        self.count = self.x_len * self.z_len * self.plane
        self.scale = 1.0 / self.count
        assert z_parts == 2 and 2 * self.width == LANES and self.group * self.xz == LANES
        assert self.zl == MZ

    def tables(self):
        bf = lambda t: np.ascontiguousarray(t).astype(ml_dtypes.bfloat16)
        g = self.group * self.xl
        eye = np.eye(g, dtype=np.float32)
        zf = pair_table(mode_angles(self.z_len, MZ, False), False)
        zf = zf.reshape(2, self.zl, 2, MZ, 2)
        zf = np.einsum("hzplq,ab->hpazbql", zf, eye).reshape(2, 2 * LANES, 2 * LANES)
        z_forward = np.stack([np.concatenate([zf[0], zf[1]], 0), np.concatenate([zf[1], zf[0]], 0)])
        zi = pair_table(mode_angles(self.z_len, MZ, False), True)
        zi = zi.reshape(2, self.zl, 2, MZ, 2)
        zi = np.einsum("hzplq,ab->hqazbpl", zi, eye).reshape(2, 2 * LANES, 2 * LANES)
        z_inverse = np.stack([np.concatenate([zi[1], zi[0]], 0), np.concatenate([zi[0], zi[1]], 0)])
        eye = np.eye(MZ, dtype=np.float32)
        xf = pair_table(mode_angles(self.x_len, MX, False), False)
        xf = xf.reshape(self.x_len, 2, 2, self.kxl, 2)
        x_forward = np.einsum("xpjkr,ab->jrxpakb", xf, eye)
        x_forward = x_forward.reshape(2, 2, self.xp * self.width, self.modes)
        xi = pair_table(mode_angles(self.x_len, MX, False), True)
        xi = xi.reshape(self.x_len, 2, 2, self.kxl, 2)
        x_inverse = np.einsum("xrjkq,ab->jrkaxqb", xi, eye)
        x_inverse = x_inverse.reshape(2, 2, self.modes, self.xp * self.width)
        owner = np.repeat(np.eye(self.chans, dtype=np.float32), self.xz, axis=0)
        return dict(
            plane=bf(plane_rows()),
            z_forward=bf(z_forward),
            z_inverse=bf(z_inverse),
            x_forward=bf(x_forward),
            x_inverse=bf(x_inverse),
            owner=bf(owner),
        )


def params(**kw):
    return pltpu.CompilerParams(vmem_limit_bytes=VMEM_LIMIT, **kw)


def cost(flops, nbytes):
    return pl.CostEstimate(flops=int(flops), bytes_accessed=int(nbytes), transcendentals=0)


def hbm(value):
    return pltpu.with_memory_space_constraint(value, pltpu.HBM)


def vmem(value):
    return pltpu.with_memory_space_constraint(value, pltpu.VMEM)


WHOLE = pl.BlockSpec(memory_space=pltpu.VMEM)
SCALAR = pl.BlockSpec(memory_space=pltpu.SMEM)
ANYWHERE = pl.BlockSpec(memory_space=pl.ANY)


def shape(dims, kind=BF):
    return jax.ShapeDtypeStruct(tuple(dims), kind)


def full(dims):
    return pl.BlockSpec(tuple(dims), lambda *_: (0,) * len(dims))


def dot(a, b):
    return lax.dot_general(a, b, (((1,), (0,)), ((), ())), preferred_element_type=F32)


def dot_t(a, b):
    return lax.dot_general(a, b, (((1,), (1,)), ((), ())), preferred_element_type=F32)


def pad_lanes(plan, out_ref):
    if plan.rows_pad > plan.rows:
        pad = plan.rows_pad - plan.rows
        out_ref[:, plan.rows :] = jnp.zeros((2 * plan.ms, pad), BF)


def half_rows(plan, half):
    return pl.ds(pl.multiple_of(2 * plan.ms + half * plan.rows, math.gcd(2 * plan.ms, plan.rows)), plan.rows)


def mix_masks(plan, owned_ref, mask_ref, wide_ref):
    cells = 2 * plan.rows
    shift = plan.xz.bit_length() - 1
    assert 1 << shift == plan.xz
    iota = lambda dims, axis: lax.broadcasted_iota(jnp.int32, dims, axis)
    mine = (iota((plan.chans, cells), 1) >> shift) == iota((plan.chans, cells), 0)
    owned_ref[...] = jnp.where(mine, 1.0, 0.0).astype(BF)
    apart = (iota((plan.xz, cells), 0) - iota((plan.xz, cells), 1)) & (plan.xz - 1)
    mask_ref[...] = jnp.where(apart == 0, 1.0, 0.0).astype(F32)


def mix_matrix(plan, mix, back, owned_ref, mask_ref, wide_ref, out_ref):
    sides = (((1,), (0,)), ((), ())) if back else (((0,), (0,)), ((), ()))
    wide_ref[...] = lax.dot_general(mix, owned_ref[...], sides, preferred_element_type=F32)
    for c in range(plan.chans):
        half, start = c // plan.half, (c % plan.half) * plan.xz
        line = wide_ref[c : c + 1, :] * mask_ref[...]
        out_ref[half, start : start + plan.xz, :] = line.astype(BF)


def mix_scratch(plan):
    cells = 2 * plan.rows
    return [pltpu.VMEM((plan.chans, cells), BF), pltpu.VMEM((plan.xz, cells), F32), pltpu.VMEM((plan.chans, cells), F32)]


def load_forward(plan, me, field, plane, mix):
    tiles = 2
    width = plan.plane // tiles
    ms2 = 2 * plan.ms
    cells = 2 * plan.rows

    def kernel(
        me_ref, field_ref, plane_ref, mix_ref, stack_ref, out_ref, mixing_ref,
        acc, small, sems, mix_sem, *masks,
    ):
        me = me_ref[0]
        copies = []
        for k in range(tiles):
            at = slice(k * width, (k + 1) * width)
            copies.append(
                (
                    pltpu.make_async_copy(plane_ref.at[:, at], stack_ref.at[:ms2, at], sems.at[0, k]),
                    pltpu.make_async_copy(
                        field_ref.at[1 - me, :, at], stack_ref.at[half_rows(plan, 1 - me), at], sems.at[1, k]
                    ),
                    pltpu.make_async_copy(
                        field_ref.at[me, :, at], stack_ref.at[half_rows(plan, me), at], sems.at[2, k]
                    ),
                )
            )
        mix_load = pltpu.make_async_copy(mix_ref, small, mix_sem)
        mix_load.start()
        for group in copies:
            group[0].start()
            group[1].start()
        for group in copies:
            group[2].start()
        mix_masks(plan, *masks)
        for k, group in enumerate(copies):
            at = slice(k * width, (k + 1) * width)
            group[0].wait()
            group[1].wait()
            value = dot_t(stack_ref[:ms2, at], stack_ref[half_rows(plan, 1 - me), at])
            if k == 0:
                acc[...] = value
            else:
                acc[...] += value
        pad_lanes(plan, out_ref)
        out_ref[:, : plan.rows] = acc[...].astype(BF)
        mix_load.wait()
        mix_matrix(plan, small[...], False, *masks, mixing_ref)
        for group in copies:
            group[2].wait()

    matrix = pltpu.VMEM((2, plan.rows, cells), BF)
    return pl.pallas_call(
        kernel,
        in_specs=[SCALAR, ANYWHERE, ANYWHERE, ANYWHERE],
        out_specs=[WHOLE, WHOLE, WHOLE],
        out_shape=[pltpu.VMEM((ms2 + cells, plan.plane), BF), shape((ms2, plan.rows_pad)), matrix],
        scratch_shapes=[
            pltpu.VMEM((ms2, plan.rows), F32),
            pltpu.VMEM((plan.chans, plan.chans), BF),
            pltpu.SemaphoreType.DMA((3, tiles)),
            pltpu.SemaphoreType.DMA,
        ]
        + mix_scratch(plan),
        compiler_params=params(),
        cost_estimate=cost(4 * plan.ms * plan.rows * plan.plane, 5e6),
        name="load_forward",
    )(me, hbm(field.reshape(2, plan.rows, plan.plane)), hbm(plane), hbm(mix))


def plane_forward(plan, me, stack, spec_weight):
    ms2 = 2 * plan.ms
    tiles = 4
    native = spec_weight.transpose(1, 2, 3, 0, 4)
    step = plan.chans // tiles

    def kernel(me_ref, stack_ref, weight_in, out_ref, weight_ref, sems):
        loads = []
        for k in range(tiles):
            at = slice(k * step, (k + 1) * step)
            loads.append(pltpu.make_async_copy(weight_in.at[at], weight_ref.at[at], sems.at[k]))
            loads[-1].start()
        value = dot_t(stack_ref[:ms2, :], stack_ref[half_rows(plan, me_ref[0]), :])
        pad_lanes(plan, out_ref)
        out_ref[:, : plan.rows] = value.astype(BF)
        for load in loads:
            load.wait()

    keep, native = pl.pallas_call(
        kernel,
        in_specs=[SCALAR, WHOLE, ANYWHERE],
        out_specs=[WHOLE, WHOLE],
        out_shape=[shape((ms2, plan.rows_pad)), pltpu.VMEM(native.shape, BF)],
        scratch_shapes=[pltpu.SemaphoreType.DMA((tiles,))],
        compiler_params=params(),
        cost_estimate=cost(4 * plan.ms * plan.rows * plan.plane, 3e6),
        name="plane_forward",
    )(me, vmem(stack), hbm(native))
    return keep, native.transpose(3, 0, 1, 2, 4)


def z_forward(plan, me, own, got, table):
    def kernel(_, own_ref, got_ref, table_ref, out_ref, lines, pieces):
        ms = plan.ms
        for g in range(plan.pairs):
            at = slice(g * LANES, (g + 1) * LANES)
            parts = [own_ref[:ms, at], own_ref[ms:, at], got_ref[:ms, at], got_ref[ms:, at]]
            value = dot(jnp.concatenate(parts, 1), table_ref[0])
            for b in (0, 1):
                if 2 * g + b < plan.blocks:
                    lines[2 * g + b] = value[:, b * LANES : (b + 1) * LANES]
        pad = plan.chunk - plan.used
        for i in range(plan.xp):
            for b in range(plan.blocks):
                pieces[i, b * plan.s : (b + 1) * plan.s, :] = lines[b, i * plan.s : (i + 1) * plan.s, :]
            pieces[i, plan.used :, :] = jnp.zeros((pad, LANES), F32)
            out_ref[i] = pieces[i].astype(BF)

    side = (2 * plan.ms, plan.rows_pad)
    return pl.pallas_call(
        kernel,
        grid_spec=pltpu.PrefetchScalarGridSpec(
            num_scalar_prefetch=1,
            grid=(1,),
            in_specs=[
                full(side),
                full(side),
                pl.BlockSpec((1, 4 * LANES, 2 * LANES), lambda t, j: (j[0], 0, 0)),
            ],
            out_specs=full((plan.xp, plan.chunk, LANES)),
            scratch_shapes=[
                pltpu.VMEM((plan.blocks, plan.ms, LANES), F32),
                pltpu.VMEM((plan.xp, plan.chunk, LANES), F32),
            ],
        ),
        out_shape=shape((plan.xp, plan.chunk, LANES)),
        compiler_params=params(),
        cost_estimate=cost(3e8, 1e6),
        name="z_forward",
    )(me, own, got, table)


def x_forward(plan, me, chunks, table):
    def kernel(me_ref, in_ref, table_ref, send_ref, keep_ref, lhs, lines):
        w = plan.width
        for i in range(0, plan.xp, 2):
            first, second = in_ref[i], in_ref[i + 1]
            at = slice(i * w, (i + 2) * w)
            lhs[: plan.chunk, at] = jnp.concatenate([first[:, :w], second[:, :w]], 1)
            lhs[plan.chunk :, at] = jnp.concatenate([first[:, w:], second[:, w:]], 1)
        me = me_ref[0]
        for slot, half, out_ref in ((0, 1 - me, send_ref), (1, me, keep_ref)):
            for r in (0, 1):
                lines[slot, r] = dot(lhs[...], table_ref[half, r])
                for c in range(plan.half):
                    start = (c % 2) * plan.chunk + (c // 2) * plan.s
                    out_ref[c, r] = lines[slot, r, start : start + plan.s, :].astype(BF)

    out = (plan.half, 2, plan.s, plan.modes)
    return pl.pallas_call(
        kernel,
        grid_spec=pltpu.PrefetchScalarGridSpec(
            num_scalar_prefetch=1,
            grid=(1,),
            in_specs=[full((plan.xp, plan.chunk, LANES)), full(table.shape)],
            out_specs=[full(out), full(out)],
            scratch_shapes=[
                pltpu.VMEM((2 * plan.chunk, plan.xp * plan.width), BF),
                pltpu.VMEM((2, 2, 2 * plan.chunk, plan.modes), F32),
            ],
        ),
        out_shape=[shape(out), shape(out)],
        compiler_params=params(),
        cost_estimate=cost(3e8, 3e6),
        name="x_forward",
    )(me, chunks, table)


def mode_product(plan, me, mine, weight, own, got, adjoint):
    def kernel(me_ref, weight_ref, own_ref, got_ref, out_ref, held):
        me = me_ref[0]
        held[me] = own_ref[...].astype(F32)
        held[1 - me] = got_ref[...].astype(F32)
        start = (me if mine else 1 - me) * plan.half

        def one(k, carry):
            real = jnp.zeros((plan.s, plan.modes), F32)
            imag = jnp.zeros((plan.s, plan.modes), F32)
            for c in range(plan.chans):
                pos = (start + k, c) if adjoint else (c, start + k)
                wr = weight_ref[0, pos[0], pos[1]].astype(F32)
                wi = weight_ref[1, pos[0], pos[1]].astype(F32)
                mr = held[c // plan.half, c % plan.half, 0]
                mi = held[c // plan.half, c % plan.half, 1]
                if adjoint:
                    real += wr * mr + wi * mi
                    imag += wr * mi - wi * mr
                else:
                    real += wr * mr - wi * mi
                    imag += wr * mi + wi * mr
            out_ref[k, 0] = real.astype(BF)
            out_ref[k, 1] = imag.astype(BF)
            return carry

        lax.fori_loop(0, plan.half, one, 0)

    side = (plan.half, 2, plan.s, plan.modes)
    return pl.pallas_call(
        kernel,
        in_specs=[SCALAR, WHOLE, WHOLE, WHOLE],
        out_specs=WHOLE,
        out_shape=shape(side),
        scratch_shapes=[pltpu.VMEM((2,) + side, F32)],
        compiler_params=params(),
        cost_estimate=cost(2e9, 4e6),
        name="mode_product",
    )(me, vmem(weight), own, got)


def x_inverse(plan, me, own, got, table, mix):
    carry = mix is not None

    def kernel(me_ref, own_ref, got_ref, table_ref, *rest):
        mix_ref = rest[0] if carry else None
        out_ref, lhs, spare = rest[1:] if carry else rest
        me = me_ref[0]
        pad = plan.chunk - plan.used
        for slot, in_ref in ((0, own_ref), (1, got_ref)):
            for r in (0, 1):
                for c in range(plan.half):
                    start = (c % 2) * plan.chunk + (c // 2) * plan.s
                    lhs[slot, r, start : start + plan.s, :] = in_ref[c, r].astype(F32)
                for c in (0, 1):
                    start = c * plan.chunk + plan.used
                    lhs[slot, r, start : start + pad, :] = jnp.zeros((pad, plan.modes), F32)
        value = None
        for slot, half in ((0, me), (1, 1 - me)):
            for r in (0, 1):
                term = dot(lhs[slot, r].astype(BF), table_ref[half, r])
                value = term if value is None else value + term
        w = plan.width
        if carry:
            spare[...] = jnp.zeros((plan.chunk, LANES), F32)
            spare[plan.used : plan.used + MIX_ROWS, :] = mix_ref[...]
        for i in range(plan.xp):
            first = value[: plan.chunk, i * w : (i + 1) * w]
            second = value[plan.chunk :, i * w : (i + 1) * w]
            piece = jnp.concatenate([first, second], 1)
            if carry:
                piece = piece + spare[...]
            out_ref[i] = piece.astype(BF)

    side = (plan.half, 2, plan.s, plan.modes)
    extra = [full((MIX_ROWS, LANES))] if carry else []
    return pl.pallas_call(
        kernel,
        grid_spec=pltpu.PrefetchScalarGridSpec(
            num_scalar_prefetch=1,
            grid=(1,),
            in_specs=[full(side), full(side), full(table.shape)] + extra,
            out_specs=full((plan.xp, plan.chunk, LANES)),
            scratch_shapes=[
                pltpu.VMEM((2, 2, 2 * plan.chunk, plan.modes), F32),
                pltpu.VMEM((plan.chunk, LANES), F32),
            ],
        ),
        out_shape=shape((plan.xp, plan.chunk, LANES)),
        compiler_params=params(),
        cost_estimate=cost(3e8, 3e6),
        name="x_inverse",
    )(me, own, got, table, *([mix] if carry else []))


def z_inverse(plan, me, chunks, table, carry):
    def kernel(_, in_ref, table_ref, send_ref, keep_ref, *rest):
        mix_ref = rest[0] if carry else None
        lines, pieces = rest[-2:]
        s, ms = plan.s, plan.ms
        for i in range(plan.xp):
            pieces[i] = in_ref[i].astype(F32)
            for b in range(plan.blocks):
                lines[b, i * s : (i + 1) * s, :] = pieces[i, b * s : (b + 1) * s, :]
        for g in range(plan.pairs):
            first = lines[2 * g].astype(BF)
            if 2 * g + 1 < plan.blocks:
                second = lines[2 * g + 1].astype(BF)
            else:
                second = jnp.zeros((ms, LANES), BF)
            value = dot_t(table_ref[0], jnp.concatenate([first, second], 1))
            rows = min(LANES, plan.rows - g * LANES)
            for slot, out_ref in ((0, send_ref), (1, keep_ref)):
                start = 2 * slot * LANES
                both = [value[start : start + rows], value[start + LANES : start + LANES + rows]]
                both = jnp.concatenate(both, 1) * plan.scale
                out_ref[g * LANES : g * LANES + rows, :] = both.astype(BF)
        if carry:
            total = pieces[0, plan.used : plan.used + MIX_ROWS, :]
            for i in range(1, plan.xp):
                total = total + pieces[i, plan.used : plan.used + MIX_ROWS, :]
            mix_ref[...] = total
            high = total.astype(BF).astype(F32)
            fill = jnp.zeros((16 - 2 * MIX_ROWS, LANES), F32)
            send_ref[plan.rows :, :] = jnp.zeros((16, 2 * ms), BF)
            send_ref[plan.rows :, :LANES] = jnp.concatenate([high, total - high, fill], 0).astype(BF)

    out = (plan.rows, 2 * plan.ms)
    sent = (plan.rows + 16, 2 * plan.ms) if carry else out
    outs = [sent, out]
    out_shape = [shape(sent), shape(out)]
    if carry:
        outs.append((MIX_ROWS, LANES))
        out_shape.append(shape((MIX_ROWS, LANES), F32))
    return pl.pallas_call(
        kernel,
        grid_spec=pltpu.PrefetchScalarGridSpec(
            num_scalar_prefetch=1,
            grid=(1,),
            in_specs=[
                full((plan.xp, plan.chunk, LANES)),
                pl.BlockSpec((1, 4 * LANES, 2 * LANES), lambda t, j: (j[0], 0, 0)),
            ],
            out_specs=[full(o) for o in outs],
            scratch_shapes=[
                pltpu.VMEM((plan.blocks, plan.ms, LANES), F32),
                pltpu.VMEM((plan.xp, plan.chunk, LANES), F32),
            ],
        ),
        out_shape=out_shape,
        compiler_params=params(),
        cost_estimate=cost(3e8, 1e6),
        name="z_inverse",
    )(me, chunks, table)


def tile_loads(plan, tiles, source, target, sems):
    width = plan.plane // tiles
    groups = []
    for k in range(tiles):
        at = slice(k * width, (k + 1) * width)
        rows = [slice(h * plan.rows, (h + 1) * plan.rows) for h in (0, 1)]
        groups.append(
            [pltpu.make_async_copy(source.at[h, :, at], target.at[rows[h], at], sems.at[h, k]) for h in (0, 1)]
        )
    return groups


def gelu_slope(pre):
    size = jnp.abs(pre)
    bell = jnp.exp2(pre * pre * (-0.5 / math.log(2.0)))
    t = 1.0 / (1.0 + size * (0.3275911 / math.sqrt(2.0)))
    poly = 0.5 * 1.061405429
    for coef in (-1.453152027, 1.421413741, -0.284496736, 0.254829592):
        poly = poly * t + 0.5 * coef
    low = bell * (poly * t - size * (1.0 / math.sqrt(2.0 * math.pi)))
    return jnp.where(pre < 0.0, low, 1.0 - low)


def cells_forward(plan, me, modes, mixing, stack, cotangent, before):
    tiles = 2
    width = plan.plane // tiles
    stripe = 32
    ms2 = 2 * plan.ms
    first = before is None

    def kernel(me_ref, modes_ref, mix_ref, stack_ref, cot_ref, *rest):
        if first:
            grad, out_ref, pre, acc = rest
            half = me_ref[0]
        else:
            before_ref, grad_ref, out_ref, grad, pre, acc, sems = rest
            half = 1 - me_ref[0]
            stores = [pltpu.make_async_copy(before_ref, grad_ref.at[1 - half], sems.at[tiles])]
            stores[0].start()
        lhs = jnp.concatenate([modes_ref[...], mix_ref[half]], 1)

        def product(k):
            pre[k % 2] = dot(lhs, stack_ref[:, k * width : (k + 1) * width])

        def slope(k):
            at = slice(k * width, (k + 1) * width)
            for r in range(0, plan.rows, stripe):
                rows = slice(r, r + stripe)
                value = cot_ref[half, rows, at].astype(F32) * gelu_slope(pre[k % 2, rows, :])
                grad[rows, at] = value.astype(BF)
            if not first:
                stores.append(pltpu.make_async_copy(grad.at[:, at], grad_ref.at[half, :, at], sems.at[k]))
                stores[-1].start()

        def transform(k):
            at = slice(k * width, (k + 1) * width)
            value = dot_t(stack_ref[:ms2, at], grad[:, at])
            if k == 0:
                acc[...] = value
            else:
                acc[...] += value

        product(0)
        for k in range(tiles):
            if k + 1 < tiles:
                product(k + 1)
            slope(k)
            if k > 0:
                transform(k - 1)
        transform(tiles - 1)
        pad_lanes(plan, out_ref)
        out_ref[:, : plan.rows] = acc[...].astype(BF)
        if not first:
            for store in stores:
                store.wait()

    out = (ms2, plan.rows_pad)
    cells = (2, plan.rows, plan.plane)
    half = pltpu.VMEM((plan.rows, plan.plane), BF)
    return pl.pallas_call(
        kernel,
        in_specs=[SCALAR] + [WHOLE] * (4 if first else 5),
        out_specs=[WHOLE, WHOLE] if first else [ANYWHERE, WHOLE, WHOLE],
        out_shape=[half, shape(out)] if first else [pltpu.HBM(cells, BF), shape(out), half],
        scratch_shapes=[pltpu.VMEM((2, plan.rows, width), F32), pltpu.VMEM((ms2, plan.rows), F32)]
        + ([] if first else [pltpu.SemaphoreType.DMA((tiles + 1,))]),
        compiler_params=params(),
        cost_estimate=cost(3e9, 5e6),
        name="cells_forward_own" if first else "cells_forward_got",
    )(
        me, modes, vmem(mixing), vmem(stack), vmem(cotangent.reshape(cells)),
        *([] if first else [vmem(before)]),
    )


def cells_back(plan, me, modes, plane, mixing, grads, before, mix_sums):
    tiles = 4
    width = plan.plane // tiles
    per_row = plan.chans // MIX_ROWS
    lane = LANES // per_row
    first = before is None

    def kernel(me_ref, modes_ref, plane_in, mix_ref, grad_in, *rest):
        if first:
            held, grad_ref, plane_ref, matrix, sems, plane_sems, *masks = rest
            half = me_ref[0]
            loads = tile_loads(plan, tiles, grad_in, grad_ref, sems)
            for k, group in enumerate(loads):
                at = slice(k * width, (k + 1) * width)
                group.append(pltpu.make_async_copy(plane_in.at[:, at], plane_ref.at[:, at], plane_sems.at[k]))
                for copy in group:
                    copy.start()
            mix_masks(plan, *masks)
            mix_matrix(plan, mix_ref[...], True, *masks, matrix)
        else:
            before_ref, sums_ref, out_ref, mix_out, held, sums, sems = rest
            matrix = mix_ref
            grad_ref, plane_ref = grad_in, plane_in
            half = 1 - me_ref[0]
            stores = [pltpu.make_async_copy(before_ref, out_ref.at[1 - half], sems.at[tiles])]
            stores[0].start()
        lhs = jnp.concatenate([modes_ref[: plan.rows], matrix[half]], 1)
        for k in range(tiles):
            at = slice(k * width, (k + 1) * width)
            if first:
                for copy in loads[k]:
                    copy.wait()
            value = dot(lhs, jnp.concatenate([plane_ref[:, at], grad_ref[:, at]], 0))
            held[:, at] = value.astype(BF)
            if not first:
                stores.append(pltpu.make_async_copy(held.at[:, at], out_ref.at[half, :, at], sems.at[k]))
                stores[-1].start()
        if not first:
            sums[...] = modes_ref[plan.rows :, :LANES].astype(F32)
            total = sums_ref[...] + sums[:MIX_ROWS, :] + sums[MIX_ROWS : 2 * MIX_ROWS, :]
            for c in range(plan.chans):
                row, start = c // per_row, (c % per_row) * lane
                mix_out[c : c + 1, :] = total[row : row + 1, start : start + plan.chans]
            for store in stores:
                store.wait()

    half = pltpu.VMEM((plan.rows, plan.plane), BF)
    whole = pltpu.VMEM((2 * plan.rows, plan.plane), BF)
    if first:
        outs = [half, whole, pltpu.VMEM(plane.shape, BF), pltpu.VMEM((2, plan.rows, 2 * plan.rows), BF)]
        out_specs = [WHOLE] * 4
        scratch = [pltpu.SemaphoreType.DMA((2, tiles)), pltpu.SemaphoreType.DMA((tiles,))] + mix_scratch(plan)
    else:
        outs = [pltpu.HBM((2, plan.rows, plan.plane), BF), shape((plan.chans, plan.chans), F32)]
        out_specs = [ANYWHERE, WHOLE]
        scratch = [half, pltpu.VMEM((16, LANES), F32), pltpu.SemaphoreType.DMA((tiles + 1,))]
    return pl.pallas_call(
        kernel,
        in_specs=[SCALAR, WHOLE, ANYWHERE, WHOLE, ANYWHERE] if first else [SCALAR] + [WHOLE] * 6,
        out_specs=out_specs,
        out_shape=outs,
        scratch_shapes=scratch,
        compiler_params=params(),
        cost_estimate=cost(2e9, 4e6),
        name="cells_back_own" if first else "cells_back_got",
    )(
        me, modes, hbm(plane) if first else vmem(plane), mixing if first else vmem(mixing), hbm(grads) if first else vmem(grads),
        *([] if first else [vmem(before), mix_sums]),
    )


def mix_partial(plan, me, owner, stack, grad, before):
    cells = 2 * plan.rows
    ms2 = 2 * plan.ms
    per_row = plan.chans // MIX_ROWS
    lane = LANES // per_row
    assert per_row * MIX_ROWS == plan.chans and lane > plan.chans
    factor = 1.0 / math.sqrt(plan.count)
    first = before is None

    def kernel(me_ref, owner_ref, stack_ref, grad_ref, *rest):
        acc = rest[-1] if first else rest[-2]
        acc[...] = dot_t(stack_ref[ms2:, :], grad_ref[...])
        iota = lambda axis: lax.broadcasted_iota(jnp.int32, (plan.xz, plan.rows), axis)
        apart = (iota(0) - iota(1)) & (plan.xz - 1)
        lines = []
        for c in range(plan.chans):
            part = jnp.where(apart == 0, acc[c * plan.xz : (c + 1) * plan.xz, :], 0.0)
            lines.append(jnp.sum(part, 0, keepdims=True))
        line = jnp.concatenate(lines, 0) * factor
        high = line.astype(BF)
        low = (line - high.astype(F32)).astype(BF)
        owned = owner_ref[: plan.rows, : plan.half]
        value = dot(high, owned) + dot(low, owned)
        if first:
            rest[0][...] = value
            return
        before_ref, out_ref, _, sums = rest
        swapped = me_ref[0] == 0
        sums[:, : plan.half] = jnp.where(swapped, before_ref[...], value)
        sums[:, plan.half :] = jnp.where(swapped, value, before_ref[...])
        out_ref[...] = jnp.zeros((MIX_ROWS, LANES), F32)
        for c in range(plan.chans):
            at, start = c // per_row, (c % per_row) * lane
            out_ref[at : at + 1, start : start + plan.chans] = sums[c : c + 1, :]

    return pl.pallas_call(
        kernel,
        in_specs=[SCALAR] + [WHOLE] * (3 if first else 4),
        out_specs=WHOLE,
        out_shape=shape((plan.chans, plan.half) if first else (MIX_ROWS, LANES), F32),
        scratch_shapes=[pltpu.VMEM((cells, plan.rows), F32)]
        + ([] if first else [pltpu.VMEM((plan.chans, plan.chans), F32)]),
        compiler_params=params(),
        cost_estimate=cost(2e9, 4e6),
        name="mix_partial_own" if first else "mix_partial_got",
    )(me, owner, vmem(stack), vmem(grad), *([] if first else [before]))


def weight_grad(plan, me, field_own, field_got, grad_own, grad_got):
    chans, half = plan.chans, plan.half
    block = 2

    def kernel(me_ref, fo_ref, fg_ref, go_ref, gg_ref, out_ref, plain, turned, real, imag):
        me = me_ref[0]
        step = pl.program_id(0)

        @pl.when(step == 0)
        def _():
            for core, ref in ((me, go_ref), (1 - me, gg_ref)):
                for o in range(half):
                    r, i = ref[o, 0].astype(F32), ref[o, 1].astype(F32)
                    plain[core, o, :, 0, :] = r
                    plain[core, o, :, 1, :] = i
                    turned[core, o, :, 0, :] = i
                    turned[core, o, :, 1, :] = r
            for core, ref in ((me, fo_ref), (1 - me, fg_ref)):
                for c in range(half):
                    r, i = ref[c, 0].astype(F32) * plan.scale, ref[c, 1].astype(F32) * plan.scale
                    real[core, c, :, 0, :] = r
                    real[core, c, :, 1, :] = r
                    imag[core, c, :, 0, :] = i
                    imag[core, c, :, 1, :] = -i

        for k in range(block):
            c = step * block + k
            core = (c >= half).astype(jnp.int32)
            vr, vi = real[core, c - core * half], imag[core, c - core * half]
            for o in range(chans):
                out_ref[k, o] = vr * plain[o // half, o % half] + vi * turned[o // half, o % half]

    side = (half, 2, plan.s, plan.modes)
    held = pltpu.VMEM((2, half, plan.s, 2, plan.modes), F32)
    return pl.pallas_call(
        kernel,
        grid_spec=pltpu.PrefetchScalarGridSpec(
            num_scalar_prefetch=1,
            grid=(chans // block,),
            in_specs=[full(side)] * 4,
            out_specs=pl.BlockSpec((block, chans, plan.s, 2, plan.modes), lambda t, j: (t, 0, 0, 0, 0)),
            scratch_shapes=[held] * 4,
        ),
        out_shape=shape((chans, chans, plan.s, 2, plan.modes), F32),
        compiler_params=params(),
        cost_estimate=cost(8e9, 1.3e7),
        name="weight_grad",
    )(me, field_own, field_got, grad_own, grad_got)


def local(x_parts, z_parts, field, cotangent, spec_weight, mix_weight):
    plan = Plan(field.shape, spec_weight.shape, x_parts, z_parts)
    const = {name: jnp.asarray(value) for name, value in plan.tables().items()}
    core = lax.axis_index("gz").astype(jnp.int32)
    me = core.reshape(1)
    plane = const["plane"]


    def swap(value):
        return lax.ppermute(value, "gz", [(0, 1), (1, 0)])

    def spread(chunks):
        return lax.all_to_all(chunks, "gx", split_axis=0, concat_axis=0, tiled=True)

    def to_modes(keep, got):
        chunks = spread(z_forward(plan, me, keep, got, const["z_forward"]))
        send, own = x_forward(plan, me, chunks, const["x_forward"])
        return own, swap(send)

    def product(own, got, adjoint):
        send = mode_product(plan, me, False, weight, own, got, adjoint)
        keep = mode_product(plan, me, True, weight, own, got, adjoint)
        return keep, swap(send)

    def to_cells(keep, got, mix, beside):
        chunks = spread(x_inverse(plan, me, keep, got, const["x_inverse"], mix))
        chunks, beside = lax.optimization_barrier((chunks, beside))
        outs = z_inverse(plan, me, chunks, const["z_inverse"], mix is not None)
        return outs[1], swap(outs[0]), outs[2:], beside

    stack, send, mixing = load_forward(plan, me, field, plane, mix_weight)
    got = swap(send)
    keep, weight = plane_forward(plan, me, stack, spec_weight)
    field_own, field_got = to_modes(keep, got)
    keep, got = product(field_own, field_got, False)
    keep, got, _, _ = to_cells(keep, got, None, ())
    grad_own, keep = cells_forward(plan, me, keep, mixing, stack, cotangent, None)
    grads, send, grad_got = cells_forward(plan, me, got, mixing, stack, cotangent, grad_own)
    got = swap(send)
    partial_mix = mix_partial(plan, me, const["owner"], stack, grad_own, None)
    got, partial_mix = lax.optimization_barrier((got, partial_mix))
    grad_own, got = to_modes(keep, got)
    partial_mix = mix_partial(plan, me, const["owner"], stack, grad_got, partial_mix)
    got, partial_mix = lax.optimization_barrier((got, partial_mix))
    grad_got = got
    keep, got = product(grad_own, grad_got, True)
    spec_grad = weight_grad(plan, me, field_own, field_got, grad_own, grad_got)
    keep, got, mix, spec_grad = to_cells(keep, got, partial_mix, spec_grad)
    before, grads, table, mixing = cells_back(plan, me, keep, plane, mix_weight, grads, None, None)
    field_grad, mix_grad = cells_back(plan, me, got, table, mixing, grads, before, mix[0])
    return (field_grad.reshape(field.shape), spec_grad.transpose(3, 0, 1, 2, 4), mix_grad)


def solution(mesh):
    placed = (
        P(None, ("grp", "gx"), "gz", None),
        P(None, ("grp", "gx"), "gz", None),
        P(None, None, None, "gx", "gz"),
        P(),
    )
    return jax.shard_map(
        functools.partial(local, mesh.shape["gx"], mesh.shape["gz"]),
        mesh=mesh,
        in_specs=placed,
        out_specs=(
            P(None, ("grp", "gx"), "gz", None),
            P("grp", None, None, "gx", "gz"),
            P("grp", None),
        ),
        check_vma=False,
    )
```
